32 devices in a mesh: dp: 8 (over y, x, core), seq: 4 (over z).
Axes of the slice: x: 2, y: 2, z: 4, core: 2. Of those that a mesh axis runs over, the one named last changes fastest.
Arguments:
- tokens: bfloat16 [16384, 1024], P(('dp', 'seq')), may hold values from -6 to 6
- cotangent: bfloat16 [16384, 1024], P(('dp', 'seq')), may hold values from -6 to 6
- lengths: int32 [8], P('dp'), may hold values from 1537 to 2048, as said below
- proj_z: float32 [1024, 128], P('seq'), may hold values from -0.1875 to 0.1875
- proj_v: float32 [2048, 1024], P('seq'), may hold values from -0.1875 to 0.1875
- proj_gamma: float32 [2048, 1024], P('seq'), may hold values from -0.1875 to 0.1875
- proj_phi: float32 [1024, 1024], P('seq'), may hold values from -0.1875 to 0.1875
- proj_h: float32 [1024, 1024], P('seq'), may hold values from -0.1875 to 0.1875
- proj_u: float32 [2048, 1024], P('seq'), may hold values from -0.25 to 0.25
- proj_up: float32 [4096, 1024], P('seq'), may hold values from -0.1875 to 0.1875
- proj_down: float32 [4096, 1024], P('seq'), may hold values from -0.09375 to 0.09375
- moment_z: float32 [1024, 128], P('seq'), may hold values from -224 to 224
- moment_v: float32 [2048, 1024], P('seq'), may hold values from -224 to 224
- moment_gamma: float32 [2048, 1024], P('seq'), may hold values from -224 to 224
- moment_phi: float32 [1024, 1024], P('seq'), may hold values from -224 to 224
- moment_h: float32 [1024, 1024], P('seq'), may hold values from -224 to 224
- moment_u: float32 [2048, 1024], P('seq'), may hold values from -224 to 224
- moment_up: float32 [4096, 1024], P('seq'), may hold values from -224 to 224
- moment_down: float32 [4096, 1024], P('seq'), may hold values from -224 to 224
- channel_params: float32 [1024, 67], P('seq'), may hold values from -8 to 8
- channel_moment: float32 [1024, 67], P('seq'), may hold values from -768 to 768
- query_params: float32 [128, 3], P('seq'), may hold values from -4 to 4
- query_moment: float32 [128, 3], P('seq'), may hold values from -768 to 768
Outputs:
- block_output: bfloat16 [16384, 1024], P(('dp', 'seq'))
- tokens_grad: float32 [16384, 1024], P(('dp', 'seq'))
- updated_z: float32 [1024, 128], P('seq')
- updated_v: float32 [2048, 1024], P('seq')
- updated_gamma: float32 [2048, 1024], P('seq')
- updated_phi: float32 [1024, 1024], P('seq')
- updated_h: float32 [1024, 1024], P('seq')
- updated_u: float32 [2048, 1024], P('seq')
- updated_up: float32 [4096, 1024], P('seq')
- updated_down: float32 [4096, 1024], P('seq')
- momentum_z: float32 [1024, 128], P('seq')
- momentum_v: float32 [2048, 1024], P('seq')
- momentum_gamma: float32 [2048, 1024], P('seq')
- momentum_phi: float32 [1024, 1024], P('seq')
- momentum_h: float32 [1024, 1024], P('seq')
- momentum_u: float32 [2048, 1024], P('seq')
- momentum_up: float32 [4096, 1024], P('seq')
- momentum_down: float32 [4096, 1024], P('seq')
- updated_channel: float32 [1024, 67], P('seq')
- momentum_channel: float32 [1024, 67], P('seq')
- updated_query: float32 [128, 3], P('seq')
- momentum_query: float32 [128, 3], P('seq')
The draws below stay inside these ranges and needn't reach their ends.
Inputs may be any that keep to these rules, and one draw needn't show every extreme that they name: `lengths`: one slot is full in every draw; the others end in the last 512 positions of their slot.
All inputs are finite; a program needn't handle non-finite values.
Results may differ from the reference program's by a relative error of at most 0.011.
The reference program's roundings to bfloat16 on the way count: a program that leaves them out, or rounds other values in their place, can miss the bound.
Values may be sent and summed in bfloat16 or wider, within the bound.
No kernel may reach another device: no remote copies, remote signals or barrier semaphores. Data moves between devices by JAX's collectives and lax.ppermute only.
A program may use at most 384 MiB of HBM per device.

```python
import math
import jax
import jax.numpy as jnp
from jax import lax

D = 1024
Z = 128
V = 2048
NE = 16
FF = 4096
TOK_DEV = 512
EBLK = 64
NS_STEPS = 5
GROUP = 2048
STRETCH = 1024
TOKENS = 16384
N_DP = 8


def draw_lengths(key, part):
    key = jax.random.fold_in(key, 5)
    first, second = jax.random.split(key)
    drawn = jax.random.randint(first, (N_DP,), GROUP - TOK_DEV + 1, GROUP + 1)
    chosen = jax.random.randint(second, (), 0, N_DP)
    return jnp.where(jnp.arange(N_DP) == chosen, GROUP, drawn).astype(jnp.int32)


def draw_channel_params(key, part):
    key = jax.random.fold_in(key, 11)
    keys = jax.random.split(key, 7)
    gains = 1.0 + 0.1 * jnp.clip(jax.random.normal(keys[0], (D, 2)), -4.0, 4.0)
    omega = jnp.clip(jax.random.normal(keys[1], (D, 1)), -4.0, 4.0)
    share = 0.5
    quick = jax.random.uniform(keys[2], (D, NE)) < share
    short_span = 30.0 + 20.0 * jax.random.uniform(keys[3], (D, NE))
    long_span = GROUP * (2.0 + 6.0 * jax.random.uniform(keys[4], (D, NE)))
    span = jnp.where(quick, short_span, long_span)
    rate = jnp.sqrt(2.0 / span)
    damping = 1.0 / (rate * span)
    alpha = jnp.log(rate / (1.0 - rate))
    delta = jnp.log(damping / (1.0 - damping))
    beta = jnp.clip(jax.random.normal(keys[5], (D, NE)), -4.0, 4.0)
    eta = 0.35 * jnp.clip(jax.random.normal(keys[6], (D, NE)), -4.0, 4.0)
    return jnp.concatenate([gains, omega, alpha, delta, beta, eta], axis=1).astype(jnp.float32)


def rising_rows(key, row_count, col_count, rise):
    base = 0.3 * jnp.sqrt(jnp.float32(TOKENS))
    along = jnp.arange(row_count).astype(jnp.float32) / (row_count - 1)
    factor = (1.0 + rise * along)[:, None]
    entries = jnp.clip(jax.random.normal(key, (row_count, col_count)), -4.0, 4.0)
    return (base * factor * entries).astype(jnp.float32)


def draw_channel_moment(key, part):
    key = jax.random.fold_in(key, 17)
    rise = 2.0
    return rising_rows(key, D, 3 + 4 * NE, rise)


def draw_query_moment(key, part):
    key = jax.random.fold_in(key, 23)
    rise = 2.0
    return rising_rows(key, Z, 3, rise)


def shard_levels(key, shape, cuts, smallest, largest):
    def one(position, shards_of):
        heights = jax.random.uniform(jax.random.fold_in(jax.random.fold_in(key, 6), position), (shards_of,), jnp.float32, smallest / len(cuts), largest / len(cuts))
        return jnp.repeat(jnp.exp(heights), shape[position] // shards_of).reshape((-1,) + (1,) * (len(shape) - position - 1))

    level = one(*cuts[0])
    for cut in cuts[1:]:
        level = level * one(*cut)
    return level


def noise(rng, dims, scale, reach, cuts=(), held_as=jnp.bfloat16):
    values = scale * jax.random.normal(rng, dims, jnp.float32)
    if cuts:
        values = values * shard_levels(rng, dims, cuts, -0.22, 0.18)
    return jnp.clip(values, -reach, reach).astype(held_as)


def setup_inputs(seed: int = 0) -> dict:
    streams_of = jax.random.split(jax.random.key(seed), 24)
    return {
        "tokens": noise(streams_of[0], (TOKENS, D), 1.0, 6.0, ((0, 32),)),
        "cotangent": noise(streams_of[1], (TOKENS, D), 1.0, 6.0, ((0, 32),)),
        "lengths": draw_lengths(jax.random.fold_in(streams_of[23], 71), 0),
        "proj_z": noise(streams_of[3], (D, Z), D ** -0.5, 0.1875, ((0, 4),), jnp.float32),
        "proj_v": noise(streams_of[4], (V, D), D ** -0.5, 0.1875, ((0, 4),), jnp.float32),
        "proj_gamma": noise(streams_of[5], (V, D), D ** -0.5, 0.1875, ((0, 4),), jnp.float32),
        "proj_phi": noise(streams_of[6], (D, D), D ** -0.5, 0.1875, ((0, 4),), jnp.float32),
        "proj_h": noise(streams_of[7], (D, D), D ** -0.5, 0.1875, ((0, 4),), jnp.float32),
        "proj_u": noise(streams_of[8], (V, D), (V // 4) ** -0.5, 0.25, ((0, 4),), jnp.float32),
        "proj_up": noise(streams_of[9], (FF, D), D ** -0.5, 0.1875, ((0, 4),), jnp.float32),
        "proj_down": noise(streams_of[10], (FF, D), FF ** -0.5, 0.09375, ((0, 4),), jnp.float32),
        "moment_z": noise(streams_of[11], (D, Z), (0.3 * TOKENS ** 0.5), 224.0, ((0, 4),), jnp.float32),
        "moment_v": noise(streams_of[12], (V, D), (0.3 * TOKENS ** 0.5), 224.0, ((0, 4),), jnp.float32),
        "moment_gamma": noise(streams_of[13], (V, D), (0.3 * TOKENS ** 0.5), 224.0, ((0, 4),), jnp.float32),
        "moment_phi": noise(streams_of[14], (D, D), (0.3 * TOKENS ** 0.5), 224.0, ((0, 4),), jnp.float32),
        "moment_h": noise(streams_of[15], (D, D), (0.3 * TOKENS ** 0.5), 224.0, ((0, 4),), jnp.float32),
        "moment_u": noise(streams_of[16], (V, D), (0.3 * TOKENS ** 0.5), 224.0, ((0, 4),), jnp.float32),
        "moment_up": noise(streams_of[17], (FF, D), (0.3 * TOKENS ** 0.5), 224.0, ((0, 4),), jnp.float32),
        "moment_down": noise(streams_of[18], (FF, D), (0.3 * TOKENS ** 0.5), 224.0, ((0, 4),), jnp.float32),
        "channel_params": draw_channel_params(jax.random.fold_in(streams_of[23], 71), 0),
        "channel_moment": draw_channel_moment(jax.random.fold_in(streams_of[23], 71), 0),
        "query_params": noise(streams_of[21], (Z, 3), 1.5, 4.0, ((0, 4),), jnp.float32),
        "query_moment": draw_query_moment(jax.random.fold_in(streams_of[23], 71), 0),
    }


HIGHEST = lax.Precision.HIGHEST
POLY_A = 3.4445
POLY_B = -4.775
POLY_C = 2.0315
MOMENTUM = 0.5
MATRIX_RATE = 0.5
VECTOR_RATE = 0.2

@jax.custom_vjp
def low(v):
    return lax.optimization_barrier(v.astype(jnp.bfloat16)).astype(jnp.float32)

@jax.custom_vjp
def low_back(v):
    return v

def low_keep(v):
    return (low(v), None)

def low_pass(kept, grad):
    return (grad,)

def back_keep(v):
    return (v, None)

def back_low(kept, grad):
    return (low(grad),)
low.defvjp(low_keep, low_pass)
low_back.defvjp(back_keep, back_low)

def exact_dot(left, right):
    return jnp.dot(left, right, precision=HIGHEST, preferred_element_type=jnp.float32)

def norm_rows(rows, gain):
    center = rows - lax.optimization_barrier(jnp.mean(rows, axis=-1, keepdims=True))
    spread = lax.optimization_barrier(jnp.mean(center * center, axis=-1, keepdims=True))
    return center * lax.rsqrt(spread + 1e-05) * gain

def ema_tables(alpha, delta, beta, eta, block):
    inject_rate = jax.nn.sigmoid(alpha)
    keep_rate = 1.0 - inject_rate * jax.nn.sigmoid(delta)
    steps = jnp.arange(block + 1).astype(jnp.float32)
    powers = jnp.exp(steps[:, None, None] * jnp.log(keep_rate)[None])
    inject = inject_rate * beta
    kernel = lax.optimization_barrier(jnp.sum(powers[:block] * (eta * inject)[None], axis=1))
    places = jnp.arange(block).astype(jnp.int32)
    distance = places[:, None] - places[None, :]
    toeplitz = jnp.where((distance >= 0)[:, :, None], kernel[jnp.clip(distance, 0, block - 1)], 0.0)
    return (powers, inject, toeplitz)

def ema_run(normed, omega, alpha, delta, beta, eta, start, block):
    powers, inject, toeplitz = ema_tables(alpha, delta, beta, eta, block)
    later = powers[1:] * eta[None]
    tail = powers[block - 1::-1] * inject[None]
    last = powers[block]
    pieces = normed.reshape(normed.shape[0] // block, block, normed.shape[1])

    def one_block(state, piece):
        inner = jnp.einsum('tsc,sc->tc', toeplitz, piece, precision=HIGHEST)
        carried = jnp.einsum('tjc,jc->tc', later, state, precision=HIGHEST)
        fresh = last * state + jnp.einsum('sjc,sc->jc', tail, piece, precision=HIGHEST)
        return (fresh, inner + carried)
    final, mixed = lax.scan(jax.checkpoint(one_block), start, pieces)
    return (jax.nn.silu(mixed.reshape(normed.shape) + omega * normed), final)

def attend_stretch(queries, keys, values):
    scores = low_back(exact_dot(queries, keys.T) * Z ** (-0.5))
    places = jnp.arange(queries.shape[0])
    scores = jnp.where(places[:, None] >= places[None, :], scores, -1e+30)
    top = lax.optimization_barrier(jnp.max(scores, axis=-1, keepdims=True))
    expo = jnp.exp(scores - top)
    probs = expo / lax.optimization_barrier(jnp.sum(expo, axis=-1, keepdims=True))
    return exact_dot(low(probs), values)

def layer(rows, mats, channel, query_set):
    proj_z, proj_v, proj_gamma, proj_phi, proj_h, proj_u, proj_up, proj_down = mats
    gain_one = channel[:, 0]
    gain_two = channel[:, 1]
    omega = channel[:, 2]
    alpha = channel[:, 3:3 + NE].T
    delta = channel[:, 3 + NE:3 + 2 * NE].T
    beta = channel[:, 3 + 2 * NE:3 + 3 * NE].T
    eta = channel[:, 3 + 3 * NE:3 + 4 * NE].T
    normed = norm_rows(rows, gain_one)
    normed_low = low(normed)
    values = low(jax.nn.silu(low_back(exact_dot(normed_low, proj_v.T))))
    start = jnp.zeros((NE, D), jnp.float32)
    mixed, final = ema_run(normed, omega, alpha, delta, beta, eta, start, EBLK)
    mixed_low = low(mixed)
    zed = jax.nn.silu(low_back(exact_dot(mixed_low, proj_z)))
    queries = low(zed * query_set[:, 0] + query_set[:, 1])
    keys = low(zed * query_set[:, 2])
    count = rows.shape[0] // STRETCH
    attended = lax.map(jax.checkpoint(lambda three: attend_stretch(three[0], three[1], three[2])), (queries.reshape(count, STRETCH, Z), keys.reshape(count, STRETCH, Z), values.reshape(count, STRETCH, V)))
    attended = low_back(attended.reshape(rows.shape[0], V))
    gamma = jax.nn.silu(low_back(exact_dot(mixed_low, proj_gamma.T)))
    gated = low(gamma * attended)
    phi = jax.nn.sigmoid(low_back(exact_dot(mixed_low, proj_phi)))
    cand = jax.nn.silu(low_back(exact_dot(mixed_low, proj_h) + exact_dot(gated, proj_u)))
    middle = phi * cand + (1.0 - phi) * rows
    wide = low(norm_rows(middle, gain_two))
    active = low(jax.nn.silu(low_back(exact_dot(wide, proj_up.T))))
    return middle + low_back(exact_dot(active, proj_down))

def orthogonal(moment):
    iterate = moment / (jnp.sqrt(jnp.sum(moment * moment)) + 1e-07)
    for step in range(NS_STEPS):
        gram = exact_dot(iterate.T, iterate)
        poly = POLY_B * gram + POLY_C * exact_dot(gram, gram)
        iterate = POLY_A * iterate + exact_dot(iterate, poly)
    return iterate

def reference(tokens, cotangent, lengths, proj_z, proj_v, proj_gamma, proj_phi, proj_h, proj_u, proj_up, proj_down, moment_z, moment_v, moment_gamma, moment_phi, moment_h, moment_u, moment_up, moment_down, channel_params, channel_moment, query_params, query_moment):
    mats = (proj_z, proj_v, proj_gamma, proj_phi, proj_h, proj_u, proj_up, proj_down)
    moments = (moment_z, moment_v, moment_gamma, moment_phi, moment_h, moment_u, moment_up, moment_down)
    places = jnp.arange(GROUP).astype(jnp.int32)
    keep = (places[None, :] < lengths[:, None]).astype(jnp.float32).reshape(TOKENS, 1)
    inputs = tokens.astype(jnp.float32)
    weighted = cotangent.astype(jnp.float32) * keep

    def whole(rows, mats, channel, query_set):
        low_mats = tuple((low(item) for item in mats))
        low_channel = low(channel)
        low_query = low(query_set)
        slots = rows.reshape(N_DP, GROUP, D)
        result = lax.map(jax.checkpoint(lambda slot: layer(slot, low_mats, low_channel, low_query)), slots)
        return result.reshape(TOKENS, D)
    result, pullback = jax.vjp(whole, inputs, mats, channel_params, query_params)
    tokens_grad, mat_grads, channel_grad, query_grad = pullback(weighted)
    block_output = (result * keep).astype(jnp.bfloat16)
    fans = (D, D, D, D, D, V, D, FF)
    updated = []
    renewed_all = []
    for master, moment, grad, fan in zip(mats, moments, mat_grads, fans):
        renewed = MOMENTUM * moment + grad
        renewed_all.append(renewed)
        updated.append(master - MATRIX_RATE * math.sqrt(master.shape[0] / fan) * orthogonal(renewed))
    channel_renewed = MOMENTUM * channel_moment + channel_grad
    channel_rms = jnp.sqrt(lax.optimization_barrier(jnp.mean(channel_renewed * channel_renewed, axis=0)) + 1e-06)
    channel_new = channel_params - VECTOR_RATE * channel_renewed / channel_rms
    query_renewed = MOMENTUM * query_moment + query_grad
    query_rms = jnp.sqrt(lax.optimization_barrier(jnp.mean(query_renewed * query_renewed, axis=0)) + 1e-06)
    query_new = query_params - VECTOR_RATE * query_renewed / query_rms
    return (block_output, tokens_grad, updated[0], updated[1], updated[2], updated[3], updated[4], updated[5], updated[6], updated[7], renewed_all[0], renewed_all[1], renewed_all[2], renewed_all[3], renewed_all[4], renewed_all[5], renewed_all[6], renewed_all[7], channel_new, channel_renewed, query_new, query_renewed)
```

```python
import math

import jax
import jax.numpy as jnp
from jax import lax
from jax.experimental import pallas as pl
from jax.experimental.pallas import tpu as pltpu
from jax.sharding import PartitionSpec as P

D = 1024
Z = 128
V = 2048
NE = 16
FF = 4096
NS_STEPS = 5
LANES = 128
SUBS = D // LANES

HIGH = lax.Precision.HIGH
POLY_A = 3.4445
POLY_B = -4.775
POLY_C = 2.0315
MOMENTUM = 0.5
MATRIX_RATE = 0.5
VECTOR_RATE = 0.2

SLOT = {"up": 0, "z": 1, "down": 2, "phi": 3, "g": 4, "h": 5, "u": 6, "v": 7}
NAMES = ("z", "v", "g", "phi", "h", "u", "up", "down")
FAN = {"z": D, "v": D, "g": D, "phi": D, "h": D, "u": V, "up": D, "down": FF}


def as_half(value):
    return value.astype(jnp.bfloat16)


def times_plain(left, right):
    return jnp.dot(left, right, preferred_element_type=jnp.float32)


def times_right(left, right):
    return lax.dot_general(
        left, right, (((1,), (1,)), ((), ())), preferred_element_type=jnp.float32
    )


def times_left(left, right):
    return lax.dot_general(
        left, right, (((0,), (0,)), ((), ())), preferred_element_type=jnp.float32
    )


def times_high(left, right):
    return jnp.dot(left, right, precision=HIGH, preferred_element_type=jnp.float32)


def silu_grad(value):
    sig = jax.nn.sigmoid(value)
    return sig * (1.0 + value * (1.0 - sig))


def norm_rows(rows, gain):
    center = rows - jnp.mean(rows, axis=-1, keepdims=True)
    spread = jnp.mean(center * center, axis=-1, keepdims=True)
    return center * lax.rsqrt(spread + 1e-05) * gain


def turned(x, distance):
    count = lax.axis_size("seq")
    return lax.ppermute(x, "seq", [(i, (i + distance) % count) for i in range(count)])


def others_blocks(x):
    return [turned(x, k) for k in range(1, lax.axis_size("seq"))]


def in_order(own, others):
    count, mine = lax.axis_size("seq"), lax.axis_index("seq")
    held = jnp.stack([own] + others)
    rows = [
        lax.dynamic_index_in_dim(held, lax.rem(mine - i + count, count), 0, keepdims=False)
        for i in range(count)
    ]
    return jnp.concatenate(rows, axis=0)


def own_slice(block):
    share = block.shape[0] // lax.axis_size("dp")
    return lax.dynamic_slice_in_dim(block, lax.axis_index("dp") * share, share, 0)


def gathered_weight(block):
    dp = lax.axis_size("dp")
    share = block.shape[0] // dp
    far = jnp.stack(others_blocks(own_slice(block)))
    far = lax.all_gather(far, "dp", axis=0, tiled=False)
    near = block.reshape(dp, 1, share, block.shape[1])
    return jnp.concatenate([near, far], axis=1).reshape(-1, block.shape[1])


def summed_share(grad):
    count = lax.axis_size("seq")
    dp = lax.axis_size("dp")
    share = grad.shape[0] // (dp * count)
    part = lax.psum_scatter(grad, "dp", scatter_dimension=0, tiled=True)
    part = part.reshape(count, share, grad.shape[1])
    total = part[0].astype(jnp.float32)
    for k in range(1, count):
        total = total + turned(part[k], -k).astype(jnp.float32)
    return total


def in_columns(block, slots):
    count = lax.axis_size("seq")
    return [
        lax.ppermute(
            block,
            ("dp", "seq"),
            [(s * count + i, s * count + (i + k) % count) for s in slots for i in range(count)],
        )
        for k in range(1, count)
    ]


def summed_small(x):
    count, mine, dp = lax.axis_size("seq"), lax.axis_index("seq"), lax.axis_size("dp")
    share = x.shape[0] // count
    held = x.reshape(count, share, x.shape[1])
    total = lax.dynamic_index_in_dim(held, mine, 0, keepdims=False)
    for k in range(1, count):
        piece = lax.dynamic_index_in_dim(held, lax.rem(mine + k, count), 0, keepdims=False)
        total = total + turned(piece, k)
    step = 1
    while step < dp:
        total = total + lax.ppermute(total, "dp", [(i, i ^ step) for i in range(dp)])
        step *= 2
    return total


def ema_end_kernel(u_ref, q_ref, end_ref):
    q = [q_ref[j] for j in range(NE)]

    def step(t, state):
        u = u_ref[t]
        return tuple(q[j] * state[j] + u for j in range(NE))

    zero = jnp.zeros((SUBS, LANES), jnp.float32)
    state = lax.fori_loop(0, u_ref.shape[0], step, (zero,) * NE, unroll=8)
    for j in range(NE):
        end_ref[j] = state[j]


def ema_run_kernel(u_ref, q_ref, w_ref, start_ref, e_ref):
    q = [q_ref[j] for j in range(NE)]
    w = [w_ref[j] for j in range(NE)]

    def step(t, state):
        u = u_ref[t]
        state = tuple(q[j] * state[j] + u for j in range(NE))
        terms = [w[j] * state[j] for j in range(NE)]
        while len(terms) > 1:
            terms = [terms[i] + terms[i + 1] for i in range(0, len(terms), 2)]
        e_ref[t] = terms[0]
        return state

    lax.fori_loop(0, u_ref.shape[0], step, tuple(start_ref[j] for j in range(NE)), unroll=4)


def ema_sums_kernel(u_ref, de_ref, q_ref, start_ref, first_ref, dw_ref, dh_ref, tail_ref):
    rows = u_ref.shape[0]
    zero = jnp.zeros((SUBS, LANES), jnp.float32)
    half = NE // 2
    for base in (0, half):
        q = [q_ref[base + j] for j in range(half)]

        def step(t, carry, q=q):
            h, g, dw, dh, r = carry
            u, de, late = u_ref[t], de_ref[t], de_ref[rows - 1 - t]
            g = tuple(q[j] * g[j] + h[j] for j in range(half))
            h = tuple(q[j] * h[j] + u for j in range(half))
            dw = tuple(dw[j] + de * h[j] for j in range(half))
            dh = tuple(dh[j] + de * g[j] for j in range(half))
            r = tuple(q[j] * r[j] + late for j in range(half))
            return (h, g, dw, dh, r)

        blank = (zero,) * half
        start = tuple(start_ref[base + j] for j in range(half))
        _, g, dw, dh, r = lax.fori_loop(0, rows, step, (start, blank, blank, blank, blank), unroll=2)
        for j in range(half):
            dw_ref[base + j] = dw[j]
            dh_ref[base + j] = dh[j]
            tail_ref[base + j] = g[j]
            first_ref[base + j] = r[j]


def ema_back_kernel(de_ref, q_ref, w_ref, start_ref, du_ref):
    rows = de_ref.shape[0]
    q = [q_ref[j] for j in range(NE)]
    w = [w_ref[j] for j in range(NE)]

    def step(s, state):
        t = rows - 1 - s
        de = de_ref[t]
        state = tuple(q[j] * state[j] + de for j in range(NE))
        terms = [w[j] * state[j] for j in range(NE)]
        while len(terms) > 1:
            terms = [terms[i] + terms[i + 1] for i in range(0, len(terms), 2)]
        du_ref[t] = terms[0]
        return state

    lax.fori_loop(0, rows, step, tuple(start_ref[j] for j in range(NE)), unroll=4)


def f32_shape(*dims):
    return jax.ShapeDtypeStruct(dims, jnp.float32)


def local_call(kernel, out_shape, flops, moved, *args):
    return pl.pallas_call(
        kernel,
        out_shape=out_shape,
        compiler_params=pltpu.CompilerParams(vmem_limit_bytes=24 * 1024 * 1024),
        cost_estimate=pl.CostEstimate(flops=flops, bytes_accessed=moved, transcendentals=0),
    )(*args)


def tiled(x):
    return x.reshape(x.shape[:-1] + (SUBS, LANES))


def flat(x):
    return x.reshape(x.shape[:-2] + (D,))


def carried(ends, decay, forward):
    count, mine = lax.axis_size("seq"), lax.axis_index("seq")
    total = jnp.zeros_like(ends)
    factor = jnp.ones_like(decay)
    for k in range(1, count):
        if forward:
            pairs = [(i, i + k) for i in range(count - k)]
        else:
            pairs = [(i + k, i) for i in range(count - k)]
        total = total + factor * lax.ppermute(ends, "seq", pairs)
        factor = factor * decay
    return total


def orthogonal_factor(gram_raw):
    scale = 1.0 / (jnp.sqrt(jnp.trace(gram_raw)) + 1e-07)
    gram = gram_raw * (scale * scale)
    eye = jnp.eye(gram.shape[0], dtype=jnp.float32)
    factor = None
    for step in range(NS_STEPS):
        square = times_high(gram, gram)
        poly = POLY_A * eye + POLY_B * gram + POLY_C * square
        factor = poly * scale if factor is None else times_high(factor, poly)
        if step + 1 < NS_STEPS:
            gram = times_high(times_high(gram, poly), poly)
    return factor


def body(tokens, cotangent, lengths, *rest):
    order = ("z", "v", "g", "phi", "h", "u", "up", "down")
    masters = dict(zip(order, rest[:8]))
    moments = dict(zip(order, rest[8:16]))
    channel_params, channel_moment, query_params, query_moment = rest[16:]
    seq_count = lax.axis_size("seq")
    seq_index = lax.axis_index("seq")
    dp_count = lax.axis_size("dp")
    dp_index = lax.axis_index("dp")
    rows = tokens.shape[0]

    half = {name: as_half(masters[name]) for name in order}
    small = jnp.concatenate(
        [
            channel_params,
            jnp.pad(query_params, ((0, channel_params.shape[0] - query_params.shape[0]), (0, 0))),
        ],
        axis=1,
    )
    small = as_half(small)
    small_all = in_order(small, others_blocks(small)).astype(jnp.float32)
    channel = small_all[:, : channel_params.shape[1]]
    query_set = small_all.reshape(seq_count, -1, small_all.shape[1])[
        :, : query_params.shape[0], channel_params.shape[1] :
    ].reshape(Z, 3)
    full = {"v": gathered_weight(half["v"])}
    wide_block = jnp.concatenate([half["z"], half["phi"], half["h"]], axis=1)
    wide_full = lax.all_gather(own_slice(wide_block), ("seq", "dp"), axis=0, tiled=True)
    full["z"] = wide_full[:, :Z]
    full["phi"] = wide_full[:, Z : Z + D]
    full["h"] = wide_full[:, Z + D :]
    for name in ("g", "u", "up", "down"):
        full[name] = gathered_weight(half[name])

    gain_one = channel[:, 0]
    gain_two = channel[:, 1]
    omega = channel[:, 2]
    alpha, delta, beta, eta = (
        channel[:, 3 + k * NE : 3 + (k + 1) * NE].T for k in range(4)
    )
    scale_q = query_set[:, 0]
    shift_q = query_set[:, 1]
    scale_k = query_set[:, 2]
    score_scale = Z ** (-0.5)

    place = seq_index * rows + jnp.arange(rows, dtype=jnp.int32)
    keep = (place < lengths[0]).astype(jnp.float32)[:, None]
    inputs = tokens.astype(jnp.float32)
    weighted = cotangent.astype(jnp.float32) * keep
    back_ffn = as_half(weighted)
    normed, norm_back_one = jax.vjp(norm_rows, inputs, gain_one)
    normed_low = as_half(normed)
    evens = [(i, i + 1) for i in range(0, seq_count - 1, 2)]
    odds = [(i + 1, i) for i in range(0, seq_count - 1, 2)]
    normed_both = jnp.concatenate([lax.ppermute(normed_low, "seq", evens), normed_low], axis=0)

    inject_rate = jax.nn.sigmoid(alpha)
    damp = jax.nn.sigmoid(delta)
    decay = 1.0 - inject_rate * damp
    mix = eta * inject_rate * beta
    decay_tiled, mix_tiled = tiled(decay), tiled(mix)
    decay_all = decay_tiled**rows
    normed_tiled = tiled(normed)
    ends = local_call(
        ema_end_kernel, f32_shape(NE, SUBS, LANES), 2 * rows * NE * D, 4 * rows * D, normed_tiled, decay_tiled
    )
    start = carried(ends, decay_all, True)
    v_pre = times_right(normed_both, full["v"])
    values_all = as_half(jax.nn.silu(v_pre))
    ema = flat(
        local_call(
            ema_run_kernel,
            f32_shape(rows, SUBS, LANES),
            4 * rows * NE * D,
            8 * rows * D,
            normed_tiled,
            decay_tiled,
            mix_tiled,
            start,
        )
    )
    mix_pre = ema + omega * normed
    mixed_low = as_half(jax.nn.silu(mix_pre))
    z_pre = times_plain(mixed_low, full["z"])
    zed = jax.nn.silu(z_pre)
    queries_low = as_half(zed * scale_q + shift_q)
    keys_low = as_half(zed * scale_k)
    keys_all = jnp.concatenate([lax.ppermute(keys_low, "seq", evens), keys_low], axis=0)
    odd_device = seq_index % 2 == 1
    query_place = jnp.arange(rows)[:, None]
    key_place = jnp.arange(2 * rows)[None, :]
    allowed = jnp.where(key_place < rows, odd_device, key_place - rows <= query_place)
    scores = jnp.where(allowed, times_right(queries_low, keys_all) * score_scale, -1e30)
    top = jnp.max(scores, axis=-1, keepdims=True)
    expo = jnp.exp(scores - top)
    probs = expo / jnp.sum(expo, axis=-1, keepdims=True)
    probs_low = as_half(probs)
    attended = times_plain(probs_low, values_all)
    gam_pre = times_right(mixed_low, full["g"])
    gamma = jax.nn.silu(gam_pre)
    gated_low = as_half(gamma * attended)
    phi = jax.nn.sigmoid(times_plain(mixed_low, full["phi"]))
    h_pre = times_plain(mixed_low, full["h"]) + times_plain(gated_low, full["u"])
    cand = jax.nn.silu(h_pre)
    middle = phi * cand + (1.0 - phi) * inputs
    wide, norm_back_two = jax.vjp(norm_rows, middle, gain_two)
    wide_low = as_half(wide)
    a_pre = times_right(wide_low, full["up"])
    active_low = as_half(jax.nn.silu(a_pre))
    result = middle + times_plain(active_low, full["down"])
    block_output = as_half(result * keep)

    share = {}
    share["down"] = summed_share(as_half(times_left(active_low, back_ffn)))
    d_apre = as_half(times_right(back_ffn, full["down"]) * silu_grad(a_pre))
    share["up"] = summed_share(as_half(times_left(d_apre, wide_low)))
    d_mid_norm, d_gain_two = norm_back_two(times_plain(d_apre, full["up"]))
    d_middle = weighted + d_mid_norm
    d_phipre = as_half(d_middle * (cand - inputs) * phi * (1.0 - phi))
    d_hpre = as_half(d_middle * phi * silu_grad(h_pre))
    tokens_grad = d_middle * (1.0 - phi)
    d_gated = times_right(d_hpre, full["u"])
    d_attended = as_half(d_gated * gamma)
    d_gampre = as_half(d_gated * attended * silu_grad(gam_pre))
    share["u"] = summed_share(as_half(times_left(gated_low, d_hpre)))
    share["g"] = summed_share(as_half(times_left(d_gampre, mixed_low)))

    d_probs = times_right(d_attended, values_all)
    d_scores = as_half(probs * (d_probs - jnp.sum(probs * d_probs, axis=-1, keepdims=True)))
    d_vpre = as_half(times_left(probs_low, d_attended) * silu_grad(v_pre))
    share["v"] = summed_share(as_half(times_left(d_vpre, normed_both)))
    d_queries = times_plain(d_scores, keys_all) * score_scale
    d_keys_all = times_left(d_scores, queries_low) * score_scale
    d_keys = d_keys_all[rows:] + lax.ppermute(d_keys_all[:rows], "seq", odds)
    d_normed_all = times_plain(d_vpre, full["v"])
    d_normed = d_normed_all[rows:] + lax.ppermute(
        as_half(d_normed_all[:rows]), "seq", odds
    ).astype(jnp.float32)
    d_scale_q = jnp.sum(d_queries * zed, axis=0)
    d_shift_q = jnp.sum(d_queries, axis=0)
    d_scale_k = jnp.sum(d_keys * zed, axis=0)
    d_zpre = as_half((d_queries * scale_q + d_keys * scale_k) * silu_grad(z_pre))
    d_wide = jnp.concatenate([d_zpre, d_phipre, d_hpre], axis=1)
    grad_wide = as_half(times_left(mixed_low, d_wide))
    ordered = grad_wide.reshape(seq_count, dp_count, -1, grad_wide.shape[1])
    ordered = jnp.stack(
        [
            lax.dynamic_index_in_dim(
                ordered, lax.rem(seq_index - k + seq_count, seq_count), 0, keepdims=False
            )
            for k in range(seq_count)
        ],
        axis=1,
    )
    share_wide = summed_share(ordered.reshape(grad_wide.shape))
    share["z"] = share_wide[:, :Z]
    share["phi"] = share_wide[:, Z : Z + D]
    share["h"] = share_wide[:, Z + D :]
    d_mixed = times_right(d_wide, wide_full) + times_plain(d_gampre, full["g"])

    d_ema = d_mixed * silu_grad(mix_pre)
    d_ema_tiled = tiled(d_ema)
    state_shape = f32_shape(NE, SUBS, LANES)
    first, d_mix, d_state, state_tail = local_call(
        ema_sums_kernel,
        (state_shape,) * 4,
        10 * rows * NE * D,
        8 * rows * D,
        normed_tiled,
        d_ema_tiled,
        decay_tiled,
        start,
    )
    behind = carried(first, decay_all, False)
    d_normed_ema = flat(
        local_call(
            ema_back_kernel,
            f32_shape(rows, SUBS, LANES),
            4 * rows * NE * D,
            8 * rows * D,
            d_ema_tiled,
            decay_tiled,
            mix_tiled,
            behind,
        )
    )
    d_mix = flat(d_mix)
    d_decay = mix * flat(d_state + decay_tiled * behind * state_tail)
    d_eta = d_mix * inject_rate * beta
    d_beta = d_mix * eta * inject_rate
    d_inject = d_mix * eta * beta - d_decay * damp
    d_alpha = d_inject * inject_rate * (1.0 - inject_rate)
    d_delta = -d_decay * inject_rate * damp * (1.0 - damp)
    d_omega = jnp.sum(d_ema * normed, axis=0)
    d_input_norm, d_gain_one = norm_back_one(d_normed + d_normed_ema + omega * d_ema)
    tokens_grad = tokens_grad + d_input_norm

    share_low = {}
    momentum = {}
    for name in order:
        share_low[name] = as_half(MOMENTUM * own_slice(moments[name]) + share[name])
    block = {}
    for name in ("down", "up", "u", "g", "phi", "h"):
        block[name] = lax.all_gather(share_low[name], "dp", axis=0, tiled=True)
        momentum[name] = block[name].astype(jnp.float32)

    def chosen(names, height):
        out = jnp.zeros((height, D), jnp.bfloat16)
        for name in names:
            item = block[name]
            item = jnp.pad(item, ((0, height - item.shape[0]), (0, D - item.shape[1])))
            out = jnp.where(dp_index == SLOT[name], item, out)
        return out

    def gram_of(names):
        height = max(block[name].shape[0] for name in names)
        own = chosen(names, height)
        pieces = [own] + in_columns(own, [SLOT[name] for name in names])
        return times_left(jnp.concatenate(pieces, axis=0), jnp.concatenate(pieces, axis=0))

    gram = gram_of(("down", "up")) + gram_of(("u", "g", "phi", "h"))
    late = jnp.concatenate([share_low["v"], share_low["z"].reshape(-1, D)], axis=0)
    late = lax.all_gather(late, ("seq", "dp"), axis=0, tiled=False)
    late = late.reshape(seq_count, dp_count, -1, D)
    cut = share_low["v"].shape[0]
    all_v = late[:, :, :cut].reshape(seq_count, -1, D)
    all_z = late[:, :, cut:].reshape(seq_count, -1, Z)
    block["v"] = lax.dynamic_index_in_dim(all_v, seq_index, 0, keepdims=False)
    block["z"] = lax.dynamic_index_in_dim(all_z, seq_index, 0, keepdims=False)
    for name in ("v", "z"):
        momentum[name] = block[name].astype(jnp.float32)
    all_v = all_v.reshape(-1, D)
    all_z = all_z.reshape(-1, Z)
    gram_v = times_left(all_v, all_v)
    gram_z = jnp.pad(times_left(all_z, all_z), ((0, D - Z), (0, D - Z)))
    gram = gram + jnp.where(dp_index == SLOT["v"], gram_v, 0.0)
    gram = gram + jnp.where(dp_index == SLOT["z"], gram_z, 0.0)
    factor = as_half(orthogonal_factor(gram))
    height = max(block[name].shape[0] for name in order)
    direction = as_half(times_plain(chosen(order, height), factor))
    directions = lax.all_gather(direction, "dp", axis=0, tiled=False)
    updated = {}
    for name in order:
        master = masters[name]
        piece = directions[SLOT[name], : master.shape[0], : master.shape[1]].astype(jnp.float32)
        rate = MATRIX_RATE * math.sqrt(master.shape[0] * seq_count / FAN[name])
        updated[name] = master - rate * piece

    grad_channel = jnp.concatenate(
        [
            d_gain_one[:, None],
            d_gain_two[:, None],
            d_omega[:, None],
            d_alpha.T,
            d_delta.T,
            d_beta.T,
            d_eta.T,
        ],
        axis=1,
    )
    grad_query = jnp.stack([d_scale_q, d_shift_q, d_scale_k], axis=1)
    query_rows = Z // seq_count
    channel_rows = D // seq_count
    grad_query = jnp.pad(
        grad_query.reshape(seq_count, query_rows, 3),
        ((0, 0), (0, channel_rows - query_rows), (0, 0)),
    ).reshape(D, 3)
    small_sum = summed_small(jnp.concatenate([grad_channel, grad_query], axis=1))
    columns = channel_params.shape[1]
    channel_renewed = MOMENTUM * channel_moment + small_sum[:, :columns]
    query_renewed = MOMENTUM * query_moment + small_sum[:query_rows, columns:]
    squares = jnp.concatenate(
        [
            jnp.sum(channel_renewed * channel_renewed, axis=0),
            jnp.sum(query_renewed * query_renewed, axis=0),
        ]
    )[None]
    squares = sum(others_blocks(squares), squares)[0]
    channel_rms = jnp.sqrt(squares[:columns] / D + 1e-06)
    channel_new = channel_params - VECTOR_RATE * channel_renewed / channel_rms
    query_rms = jnp.sqrt(squares[columns:] / Z + 1e-06)
    query_new = query_params - VECTOR_RATE * query_renewed / query_rms
    return (
        block_output,
        tokens_grad,
        *[updated[name] for name in order],
        *[momentum[name] for name in order],
        channel_new,
        channel_renewed,
        query_new,
        query_renewed,
    )


def solution(mesh):
    token_spec = P(("dp", "seq"), None)
    row_spec = P("seq", None)
    return jax.shard_map(
        body,
        mesh=mesh,
        in_specs=(token_spec, token_spec, P("dp")) + (row_spec,) * 20,
        out_specs=(token_spec, token_spec) + (row_spec,) * 20,
        check_vma=False,
    )
```

```python
import math

import jax
import jax.numpy as jnp
from jax import lax
from jax.experimental import pallas as pl
from jax.experimental.pallas import tpu as pltpu
from jax.sharding import PartitionSpec as P

D = 1024
Z = 128
V = 2048
NE = 16
FF = 4096
NS_STEPS = 5
LANES = 128
SUBS = D // LANES

POLY_A = 3.4445
POLY_B = -4.775
POLY_C = 2.0315
MOMENTUM = 0.5
MATRIX_RATE = 0.5
VECTOR_RATE = 0.2

SLOT = {"up": 0, "z": 1, "down": 2, "phi": 3, "g": 4, "h": 5, "u": 6, "v": 7}
NAMES = ("z", "v", "g", "phi", "h", "u", "up", "down")
FAN = {"z": D, "v": D, "g": D, "phi": D, "h": D, "u": V, "up": D, "down": FF}


def as_half(value):
    return value.astype(jnp.bfloat16)


def times_plain(left, right):
    return jnp.dot(left, right, preferred_element_type=jnp.float32)


def times_right(left, right):
    return lax.dot_general(
        left, right, (((1,), (1,)), ((), ())), preferred_element_type=jnp.float32
    )


def times_left(left, right):
    return lax.dot_general(
        left, right, (((0,), (0,)), ((), ())), preferred_element_type=jnp.float32
    )


def silu_grad(value):
    sig = jax.nn.sigmoid(value)
    return sig * (1.0 + value * (1.0 - sig))


def norm_rows(rows, gain):
    center = rows - jnp.mean(rows, axis=-1, keepdims=True)
    spread = jnp.mean(center * center, axis=-1, keepdims=True)
    return center * lax.rsqrt(spread + 1e-05) * gain


def turned(x, distance):
    count = lax.axis_size("seq")
    return lax.ppermute(x, "seq", [(i, (i + distance) % count) for i in range(count)])


def others_blocks(x):
    return [turned(x, k) for k in range(1, lax.axis_size("seq"))]


def in_order(own, others):
    count, mine = lax.axis_size("seq"), lax.axis_index("seq")
    held = jnp.stack([own] + others)
    rows = [
        lax.dynamic_index_in_dim(held, lax.rem(mine - i + count, count), 0, keepdims=False)
        for i in range(count)
    ]
    return jnp.concatenate(rows, axis=0)


def own_slice(block):
    share = block.shape[0] // lax.axis_size("dp")
    return lax.dynamic_slice_in_dim(block, lax.axis_index("dp") * share, share, 0)


def across(x, bit):
    return lax.ppermute(x, "dp", [(i, i ^ bit) for i in range(lax.axis_size("dp"))])


def chip_bits():
    bits = []
    bit = 2
    while bit < lax.axis_size("dp"):
        bits.append(bit)
        bit *= 2
    return bits, bits[::-1]


def own_bit(bit):
    return lax.rem(lax.axis_index("dp") // bit, 2)


def pick(x, axis, index):
    return lax.dynamic_index_in_dim(x, index, axis, keepdims=False)


def add_half(left, right):
    return as_half(left.astype(jnp.float32) + right.astype(jnp.float32))


class Flight:
    def __init__(self, make, given, beside):
        given, beside = lax.optimization_barrier((given, beside))
        self.steps = make(given)
        self.result = None
        sent, self.moving = next(self.steps)
        self.beside, _ = lax.optimization_barrier((beside, sent))

    def advance(self, beside):
        moving, beside = lax.optimization_barrier((self.moving, beside))
        try:
            sent, self.moving = self.steps.send(moving)
        except StopIteration as end:
            self.result = end.value
            return beside
        beside, _ = lax.optimization_barrier((beside, sent))
        return beside

    def finish(self):
        while self.result is None:
            try:
                _, self.moving = self.steps.send(self.moving)
            except StopIteration as end:
                self.result = end.value
        return self.result


def tied(value, beside):
    return lax.optimization_barrier((value, beside))


def near_gather(blocks):
    count = len(blocks)
    slices = blocks
    share = slices[0].shape[0] // 2
    own = jnp.concatenate([item[:share] for item in slices] + [item[share:] for item in slices], axis=0)
    others = yield [own], others_blocks(own)
    held = jnp.stack([own] + others)
    held = held.reshape(held.shape[0], 2, count, share, -1)
    orders = chip_bits()
    parts = [held[:, index][None] for index in range(2)]
    for step in reversed(range(len(orders[0]))):
        there = yield parts, [across(part, order[step]) for part, order in zip(parts, orders)]
        parts = [jnp.concatenate(pair, axis=0) for pair in zip(parts, there)]
    both = jnp.stack(parts)
    (there,) = yield [both], [across(both, 1)]
    both = jnp.stack([both, there])
    return [both[:, :, :, :, i].reshape(-1, both.shape[-1]) for i in range(count)]


def along_pieces(pieces):
    count = pieces.shape[0]
    moving = yield [pieces], [turned(pieces[k], -k) for k in range(1, count)]
    total = pieces[0].astype(jnp.float32)
    for item in moving:
        total = total + item.astype(jnp.float32)
    return total


def near_sum(grad):
    count = lax.axis_size("seq")
    middle = grad.shape[0] // 2
    (there,) = yield [grad], [across(grad[middle:], 1)]
    cut = middle // 2
    orders = chip_bits()
    parts = [
        (grad[:cut], there[:cut]),
        (grad[cut:middle], there[cut:]),
    ]
    for step in range(len(orders[0])):
        keep, send = [], []
        for mine, theirs in parts:
            rows = mine.shape[0] // 2
            send.append(add_half(mine[rows:], theirs[rows:]))
            keep.append(add_half(mine[:rows], theirs[:rows]))
        there = yield send, [across(item, order[step]) for item, order in zip(send, orders)]
        parts = list(zip(keep, there))
    pieces = jnp.concatenate(
        [add_half(mine, theirs).reshape(count, -1, mine.shape[1]) for mine, theirs in parts], axis=1
    )
    return (yield from along_pieces(pieces))


def far_gather(held):
    return lax.all_gather(held, "dp", axis=0, tiled=False).reshape(-1, held.shape[-1])


def far_sum(grad):
    count = lax.axis_size("seq")
    (part,) = yield [grad], [lax.psum_scatter(grad, "dp", scatter_dimension=0, tiled=True)]
    return (yield from along_pieces(part.reshape(count, -1, grad.shape[1])))


def whole_gather(slices):
    count, dp = lax.axis_size("seq"), lax.axis_size("dp")
    orders = chip_bits()
    others = yield slices, [others_blocks(item) for item in slices]
    parts = [in_order(own[None], [item[None] for item in rest]) for own, rest in zip(slices, others)]
    axes = [[], []]
    for step in list(reversed(range(len(orders[0])))) + [None]:
        bits = [1 if step is None else order[step] for order in orders]
        there = yield parts, [across(part, bit) for part, bit in zip(parts, bits)]
        for index, bit in enumerate(bits):
            mine = own_bit(bit) == 0
            ours, theirs = parts[index], there[index]
            parts[index] = jnp.stack([jnp.where(mine, ours, theirs), jnp.where(mine, theirs, ours)])
            axes[index].insert(0, bit)
    full = []
    for part, names in zip(parts, axes):
        bits = len(names)
        wanted = sorted(names, reverse=True)
        part = jnp.transpose(part, [bits] + [names.index(bit) for bit in wanted] + [bits + 1, bits + 2])
        full.append(part.reshape(-1, part.shape[-1]))
    return full


def whole_sum(grads):
    count, dp = lax.axis_size("seq"), lax.axis_size("dp")
    orders = chip_bits()
    mine = own_bit(1)
    parts = [jnp.swapaxes(g.reshape(count, dp // 2, 2, -1, g.shape[1]), 0, 1) for g in grads]
    send = [pick(part, 2, 1 - mine) for part in parts]
    there = yield send, [across(item, 1) for item in send]
    high = sorted(orders[0], reverse=True)
    split = (2,) * len(high)
    parts = [
        (pick(part, 2, mine).reshape(split + item.shape[1:]), item.reshape(split + item.shape[1:]))
        for part, item in zip(parts, there)
    ]
    axes = [list(high), list(high)]
    for step in range(len(high)):
        keep, send, moving = [], [], []
        for (ours, theirs), order, names in zip(parts, orders, axes):
            bit = order[step]
            axis = names.index(bit)
            names.remove(bit)
            here = own_bit(bit)
            send.append(add_half(pick(ours, axis, 1 - here), pick(theirs, axis, 1 - here)))
            keep.append(add_half(pick(ours, axis, here), pick(theirs, axis, here)))
            moving.append(across(send[-1], bit))
        there = yield send, moving
        parts = list(zip(keep, there))
    both = jnp.concatenate([add_half(ours, theirs) for ours, theirs in parts], axis=2)
    seq_index = lax.axis_index("seq")
    pieces = jnp.stack(
        [pick(both, 0, lax.rem(seq_index - k + count, count)) for k in range(count)]
    )
    return (yield from along_pieces(pieces))


def in_columns(block, slots):
    count = lax.axis_size("seq")
    up = [(s * count + i, s * count + i + 1) for s in slots for i in range(count - 1)]
    down = [(j, i) for i, j in up]
    held = [block]
    above = below = block
    for _ in range(count - 1):
        below, above = yield [below, above], [
            lax.ppermute(below, ("dp", "seq"), up),
            lax.ppermute(above, ("dp", "seq"), down),
        ]
        held += [below, above]
    return held


def summed_small(x):
    count, mine, dp = lax.axis_size("seq"), lax.axis_index("seq"), lax.axis_size("dp")
    share = x.shape[0] // count
    held = x.reshape(count, share, x.shape[1])
    total = lax.dynamic_index_in_dim(held, mine, 0, keepdims=False)
    for k in range(1, count):
        piece = lax.dynamic_index_in_dim(held, lax.rem(mine + k, count), 0, keepdims=False)
        total = total + turned(piece, k)
    step = 1
    while step < dp:
        total = total + lax.ppermute(total, "dp", [(i, i ^ step) for i in range(dp)])
        step *= 2
    return total


def ema_end_kernel(u_ref, q_ref, end_ref):
    q = [q_ref[j] for j in range(NE)]

    def step(t, state):
        u = u_ref[t]
        return tuple(q[j] * state[j] + u for j in range(NE))

    zero = jnp.zeros((SUBS, LANES), jnp.float32)
    state = lax.fori_loop(0, u_ref.shape[0], step, (zero,) * NE, unroll=8)
    for j in range(NE):
        end_ref[j] = state[j]


def ema_run_kernel(u_ref, q_ref, w_ref, start_ref, e_ref):
    q = [q_ref[j] for j in range(NE)]
    w = [w_ref[j] for j in range(NE)]

    def step(t, state):
        u = u_ref[t]
        state = tuple(q[j] * state[j] + u for j in range(NE))
        terms = [w[j] * state[j] for j in range(NE)]
        while len(terms) > 1:
            terms = [terms[i] + terms[i + 1] for i in range(0, len(terms), 2)]
        e_ref[t] = terms[0]
        return state

    lax.fori_loop(0, u_ref.shape[0], step, tuple(start_ref[j] for j in range(NE)), unroll=4)


def ema_sums_kernel(u_ref, de_ref, q_ref, start_ref, first_ref, dw_ref, dh_ref, tail_ref):
    rows = u_ref.shape[0]
    zero = jnp.zeros((SUBS, LANES), jnp.float32)
    half = NE // 2
    for base in (0, half):
        q = [q_ref[base + j] for j in range(half)]

        def step(t, carry, q=q):
            h, g, dw, dh, r = carry
            u, de, late = u_ref[t], de_ref[t], de_ref[rows - 1 - t]
            g = tuple(q[j] * g[j] + h[j] for j in range(half))
            h = tuple(q[j] * h[j] + u for j in range(half))
            dw = tuple(dw[j] + de * h[j] for j in range(half))
            dh = tuple(dh[j] + de * g[j] for j in range(half))
            r = tuple(q[j] * r[j] + late for j in range(half))
            return (h, g, dw, dh, r)

        blank = (zero,) * half
        start = tuple(start_ref[base + j] for j in range(half))
        _, g, dw, dh, r = lax.fori_loop(0, rows, step, (start, blank, blank, blank, blank), unroll=2)
        for j in range(half):
            dw_ref[base + j] = dw[j]
            dh_ref[base + j] = dh[j]
            tail_ref[base + j] = g[j]
            first_ref[base + j] = r[j]


def ema_back_kernel(de_ref, q_ref, w_ref, start_ref, du_ref):
    rows = de_ref.shape[0]
    q = [q_ref[j] for j in range(NE)]
    w = [w_ref[j] for j in range(NE)]

    def step(s, state):
        t = rows - 1 - s
        de = de_ref[t]
        state = tuple(q[j] * state[j] + de for j in range(NE))
        terms = [w[j] * state[j] for j in range(NE)]
        while len(terms) > 1:
            terms = [terms[i] + terms[i + 1] for i in range(0, len(terms), 2)]
        du_ref[t] = terms[0]
        return state

    lax.fori_loop(0, rows, step, tuple(start_ref[j] for j in range(NE)), unroll=4)


def f32_shape(*dims):
    return jax.ShapeDtypeStruct(dims, jnp.float32)


def local_call(kernel, out_shape, flops, moved, *args):
    return pl.pallas_call(
        kernel,
        out_shape=out_shape,
        compiler_params=pltpu.CompilerParams(vmem_limit_bytes=24 * 1024 * 1024),
        cost_estimate=pl.CostEstimate(flops=flops, bytes_accessed=moved, transcendentals=0),
    )(*args)


def tiled(x):
    return x.reshape(x.shape[:-1] + (SUBS, LANES))


def flat(x):
    return x.reshape(x.shape[:-2] + (D,))


def carried(ends, decay, forward):
    count, mine = lax.axis_size("seq"), lax.axis_index("seq")
    total = jnp.zeros_like(ends)
    factor = jnp.ones_like(decay)
    for k in range(1, count):
        if forward:
            pairs = [(i, i + k) for i in range(count - k)]
        else:
            pairs = [(i + k, i) for i in range(count - k)]
        total = total + factor * lax.ppermute(ends, "seq", pairs)
        factor = factor * decay
    return total


SIDE = 256


def split_half(value):
    high = value.astype(jnp.bfloat16)
    return high, (value - high.astype(jnp.float32)).astype(jnp.bfloat16)


def factor_kernel(gram_ref, high_ref, low_ref, a_ref, p_ref, t_ref, q_ref):
    side = gram_ref.shape[0]
    count = side // SIDE

    def rows_of(i):
        return slice(i * SIDE, (i + 1) * SIDE)

    def put(ref, i, strip, lead=()):
        for part, value in enumerate(split_half(strip)):
            ref[lead + (part, rows_of(i), slice(i * SIDE, side))] = value
        for j in range(i + 1, count):
            block = strip[:, (j - i) * SIDE : (j - i + 1) * SIDE].T
            for part, value in enumerate(split_half(block)):
                ref[lead + (part, rows_of(j), rows_of(i))] = value

    def strip_of(left, right, i):
        lh, ll = left[0, rows_of(i), :], left[1, rows_of(i), :]
        rh, rl = right[0, :, i * SIDE :], right[1, :, i * SIDE :]
        total = jnp.dot(lh, rl, preferred_element_type=jnp.float32)
        total = total + jnp.dot(ll, rh, preferred_element_type=jnp.float32)
        return total + jnp.dot(lh, rh, preferred_element_type=jnp.float32)

    def diagonal(i, width):
        shape = (SIDE, width)
        return lax.broadcasted_iota(jnp.int32, shape, 0) == lax.broadcasted_iota(
            jnp.int32, shape, 1
        )

    trace = jnp.zeros((1, 1), jnp.float32)
    for i in range(count):
        block = gram_ref[rows_of(i), rows_of(i)]
        block = jnp.where(diagonal(i, SIDE), block, 0.0)
        trace = trace + jnp.sum(jnp.sum(block, axis=0, keepdims=True), axis=1, keepdims=True)
    scale = 1.0 / (jnp.sqrt(trace) + 1e-07)
    for i in range(count):
        for part, value in enumerate(split_half(gram_ref[rows_of(i), :] * (scale * scale))):
            a_ref[part, rows_of(i), :] = value

    def step(k, carry):
        for i in range(count):
            width = side - i * SIDE
            now = a_ref[0, rows_of(i), i * SIDE :].astype(jnp.float32)
            now = now + a_ref[1, rows_of(i), i * SIDE :].astype(jnp.float32)
            strip = POLY_B * now + POLY_C * strip_of(a_ref, a_ref, i)
            put(p_ref, i, jnp.where(diagonal(i, width), strip + POLY_A, strip))

        @pl.when(k < NS_STEPS - 1)
        def _():
            for i in range(count):
                put(t_ref, i, strip_of(a_ref, p_ref, i))
            for i in range(count):
                put(a_ref, i, strip_of(t_ref, p_ref, i))

        there = lax.rem(k, 2)

        @pl.when(k == 0)
        def _():
            q_ref[0] = p_ref[...]

        @pl.when(k > 0)
        def _():
            for i in range(count):
                put(q_ref, i, strip_of(q_ref.at[1 - there], p_ref, i), (there,))

        return carry

    lax.fori_loop(0, NS_STEPS, step, 0)
    last = (NS_STEPS - 1) % 2
    for i in range(count):
        value = q_ref[last, 0, rows_of(i), :].astype(jnp.float32)
        value = (value + q_ref[last, 1, rows_of(i), :].astype(jnp.float32)) * scale
        high_ref[rows_of(i), :], low_ref[rows_of(i), :] = split_half(value)


def orthogonal_factor(gram):
    side = gram.shape[0]
    pair = (2, side, side)
    return pl.pallas_call(
        factor_kernel,
        out_shape=(jax.ShapeDtypeStruct(gram.shape, jnp.bfloat16),) * 2,
        scratch_shapes=[
            pltpu.VMEM(pair, jnp.bfloat16),
            pltpu.VMEM(pair, jnp.bfloat16),
            pltpu.VMEM(pair, jnp.bfloat16),
            pltpu.VMEM((2,) + pair, jnp.bfloat16),
        ],
        compiler_params=pltpu.CompilerParams(vmem_limit_bytes=56 * 1024 * 1024),
        cost_estimate=pl.CostEstimate(
            flops=17 * 4 * side**3, bytes_accessed=8 * side * side, transcendentals=0
        ),
    )(gram)


def body(tokens, cotangent, lengths, *rest):
    order = ("z", "v", "g", "phi", "h", "u", "up", "down")
    masters = dict(zip(order, rest[:8]))
    moments = dict(zip(order, rest[8:16]))
    channel_params, channel_moment, query_params, query_moment = rest[16:]
    seq_count = lax.axis_size("seq")
    seq_index = lax.axis_index("seq")
    dp_count = lax.axis_size("dp")
    dp_index = lax.axis_index("dp")
    rows = tokens.shape[0]

    half = {name: as_half(own_slice(masters[name])) for name in order}
    far_own = jnp.concatenate([half["up"], half["down"]], axis=0)
    far_held = jnp.stack([far_own] + others_blocks(far_own))
    cut = half["up"].shape[0]
    full = {"up": far_gather(far_held[:, :cut]), "down": far_gather(far_held[:, cut:])}
    small = jnp.concatenate(
        [
            channel_params,
            jnp.pad(query_params, ((0, channel_params.shape[0] - query_params.shape[0]), (0, 0))),
        ],
        axis=1,
    )
    small = as_half(small)
    small_all = in_order(small, others_blocks(small)).astype(jnp.float32)
    channel = small_all[:, : channel_params.shape[1]]
    query_set = small_all.reshape(seq_count, -1, small_all.shape[1])[
        :, : query_params.shape[0], channel_params.shape[1] :
    ].reshape(Z, 3)
    get_v = Flight(near_gather, [half["v"]], small)

    gain_one = channel[:, 0]
    gain_two = channel[:, 1]
    omega = channel[:, 2]
    alpha, delta, beta, eta = (
        channel[:, 3 + k * NE : 3 + (k + 1) * NE].T for k in range(4)
    )
    scale_q = query_set[:, 0]
    shift_q = query_set[:, 1]
    scale_k = query_set[:, 2]
    score_scale = Z ** (-0.5)

    place = seq_index * rows + jnp.arange(rows, dtype=jnp.int32)
    keep = (place < lengths[0]).astype(jnp.float32)[:, None]
    inputs = tokens.astype(jnp.float32)
    weighted = cotangent.astype(jnp.float32) * keep
    back_ffn = as_half(weighted)
    evens = [(i, i + 1) for i in range(0, seq_count - 1, 2)]
    odds = [(i + 1, i) for i in range(0, seq_count - 1, 2)]

    normed, norm_back_one = jax.vjp(norm_rows, inputs, gain_one)
    normed_low = as_half(normed)
    inject_rate = jax.nn.sigmoid(alpha)
    damp = jax.nn.sigmoid(delta)
    decay = 1.0 - inject_rate * damp
    mix = eta * inject_rate * beta
    decay_tiled, mix_tiled = tiled(decay), tiled(mix)
    decay_all = decay_tiled**rows
    normed_tiled = tiled(normed)
    ends = local_call(
        ema_end_kernel, f32_shape(NE, SUBS, LANES), 2 * rows * NE * D, 4 * rows * D, normed_tiled, decay_tiled
    )
    normed_there = lax.ppermute(normed_low, "seq", evens)
    clock = get_v.advance(ends)
    ends = clock
    zphi_slice = jnp.concatenate([half["z"], half["phi"]], axis=1)
    get_wide = Flight(whole_gather, [zphi_slice, half["h"]], clock)
    clock = get_v.advance(get_wide.beside)
    start = carried(ends, decay_all, True)
    clock = get_wide.advance(clock)
    clock = get_v.advance(clock)
    start, clock = tied(start, clock)
    ema_out = local_call(
        ema_run_kernel,
        f32_shape(rows, SUBS, LANES),
        4 * rows * NE * D,
        8 * rows * D,
        normed_tiled,
        decay_tiled,
        mix_tiled,
        start,
    )
    ema_out, clock = tied(ema_out, clock)
    clock = get_wide.advance(clock)
    clock = get_v.advance(clock)
    (full["v"],) = get_v.finish()
    normed_both = jnp.concatenate([normed_there, normed_low], axis=0)
    normed_both, clock = tied(normed_both, clock)
    v_pre = times_right(normed_both, full["v"])
    values_all = as_half(jax.nn.silu(v_pre))
    values_all, clock = tied(values_all, clock)
    clock = get_wide.advance(clock)
    get_near = Flight(near_gather, [half["g"], half["u"]], clock)
    clock = get_wide.advance(get_near.beside)
    zphi_full, full["h"] = get_wide.finish()
    full["z"], full["phi"] = zphi_full[:, :Z], zphi_full[:, Z:]
    ema_out, clock = tied(ema_out, clock)
    mix_pre = flat(ema_out) + omega * normed
    mixed_low = as_half(jax.nn.silu(mix_pre))
    z_pre = times_plain(mixed_low, full["z"])
    zed = jax.nn.silu(z_pre)
    queries_low = as_half(zed * scale_q + shift_q)
    keys_low = as_half(zed * scale_k)
    keys_there = lax.ppermute(keys_low, "seq", evens)
    phi = jax.nn.sigmoid(times_plain(mixed_low, full["phi"]))
    h_part = times_plain(mixed_low, full["h"])
    keys_there, h_part, clock = lax.optimization_barrier((keys_there, h_part, clock))
    clock = get_near.advance(clock)
    keys_all = jnp.concatenate([keys_there, keys_low], axis=0)
    odd_device = seq_index % 2 == 1
    query_place = jnp.arange(rows)[:, None]
    key_place = jnp.arange(2 * rows)[None, :]
    allowed = jnp.where(key_place < rows, odd_device, key_place - rows <= query_place)
    queries_low, clock = tied(queries_low, clock)
    scores = jnp.where(allowed, times_right(queries_low, keys_all) * score_scale, -1e30)
    top = jnp.max(scores, axis=-1, keepdims=True)
    expo = jnp.exp(scores - top)
    probs = expo / jnp.sum(expo, axis=-1, keepdims=True)
    probs_low = as_half(probs)
    attended = times_plain(probs_low, values_all)
    attended, clock = tied(attended, clock)
    clock = get_near.advance(clock)
    clock = get_near.advance(clock)
    clock = get_near.advance(clock)
    full["g"], full["u"] = get_near.finish()
    mixed_low, clock = tied(mixed_low, clock)
    gam_pre = times_right(mixed_low, full["g"])
    gamma = jax.nn.silu(gam_pre)
    gated_low = as_half(gamma * attended)
    h_pre = h_part + times_plain(gated_low, full["u"])
    cand = jax.nn.silu(h_pre)
    middle = phi * cand + (1.0 - phi) * inputs
    wide, norm_back_two = jax.vjp(norm_rows, middle, gain_two)
    wide_low = as_half(wide)
    a_pre = times_right(wide_low, full["up"])
    active_low = as_half(jax.nn.silu(a_pre))
    result = middle + times_plain(active_low, full["down"])
    block_output = as_half(result * keep)

    def share_of(name, total):
        return as_half(MOMENTUM * own_slice(moments[name]) + total)

    def kept_rows(shares):
        packed = jnp.concatenate([item.reshape(-1, D) for item in shares], axis=0)
        (packed,) = yield [packed], [lax.all_gather(packed, "dp", axis=0, tiled=False)]
        out, at = [], 0
        for item in shares:
            size = item.size // D
            out.append(packed[:, at : at + size].reshape(-1, item.shape[1]))
            at += size
        return out

    def column_rows(names, blocks):
        height = max(item.shape[0] for item in blocks)
        own = chosen(names, blocks, height)
        held = yield from in_columns(own, [SLOT[name] for name in names])
        mine = held[0]
        rest = []
        for k in range(1, seq_count):
            rest.append(held[2 * k - 1] + held[2 * (seq_count - k)])
        return jnp.concatenate([mine] + rest, axis=0)

    def chosen(names, blocks, height):
        out = jnp.zeros((height, D), jnp.bfloat16)
        for name, item in zip(names, blocks):
            item = jnp.pad(item, ((0, height - item.shape[0]), (0, D - item.shape[1])))
            out = jnp.where(dp_index == SLOT[name], item, out)
        return out

    block = {}
    orders = chip_bits()

    clock = result
    grad = as_half(times_left(active_low, back_ffn))
    sum_down = Flight(far_sum, grad, clock)
    back_ffn, clock = tied(back_ffn, sum_down.beside)
    d_apre = as_half(times_right(back_ffn, full["down"]) * silu_grad(a_pre))
    d_apre, clock = tied(d_apre, clock)
    grad = as_half(times_left(d_apre, wide_low))
    sum_up = Flight(far_sum, grad, clock)
    clock = sum_up.beside
    d_apre, clock = tied(d_apre, clock)
    d_mid_norm, d_gain_two = norm_back_two(times_plain(d_apre, full["up"]))
    d_middle = weighted + d_mid_norm
    d_phipre = as_half(d_middle * (cand - inputs) * phi * (1.0 - phi))
    d_hpre = as_half(d_middle * phi * silu_grad(h_pre))
    tokens_grad = d_middle * (1.0 - phi)
    d_hpre, clock = tied(d_hpre, clock)
    grad = as_half(times_left(gated_low, d_hpre))
    sum_u = Flight(near_sum, grad, clock)
    d_hpre, clock = tied(d_hpre, sum_u.beside)
    d_gated = times_right(d_hpre, full["u"])
    d_attended = as_half(d_gated * gamma)
    d_gampre = as_half(d_gated * attended * silu_grad(gam_pre))
    d_gampre, clock = tied(d_gampre, clock)
    clock = sum_u.advance(clock)
    d_gampre, clock = tied(d_gampre, clock)
    grad = as_half(times_left(d_gampre, mixed_low))
    sum_g = Flight(near_sum, grad, clock)
    d_attended, clock = tied(d_attended, sum_g.beside)
    d_probs = times_right(d_attended, values_all)
    d_scores = as_half(probs * (d_probs - jnp.sum(probs * d_probs, axis=-1, keepdims=True)))
    d_scores, clock = tied(d_scores, clock)
    clock = sum_g.advance(clock)
    d_attended, clock = tied(d_attended, clock)
    d_vpre = as_half(times_left(probs_low, d_attended) * silu_grad(v_pre))
    d_vpre, clock = tied(d_vpre, clock)
    clock = sum_down.advance(clock)
    clock = sum_u.advance(clock)
    d_vpre, clock = tied(d_vpre, clock)
    grad = as_half(times_left(d_vpre, normed_both))
    sum_v = Flight(near_sum, grad, clock)
    d_vpre, clock = tied(d_vpre, sum_v.beside)
    d_queries = times_plain(d_scores, keys_all) * score_scale
    d_keys_all = times_left(d_scores, queries_low) * score_scale
    d_keys_there = lax.ppermute(d_keys_all[:rows], "seq", odds)
    d_normed_all = times_plain(d_vpre, full["v"])
    d_normed_there = lax.ppermute(as_half(d_normed_all[:rows]), "seq", odds)
    d_normed_all, clock = tied(d_normed_all, clock)
    clock = sum_v.advance(clock)
    clock = sum_g.advance(clock)
    clock = sum_down.advance(clock)
    keep_down = Flight(kept_rows, [share_of("down", sum_down.finish())], clock)
    clock = sum_up.advance(keep_down.beside)
    d_keys_there, clock = tied(d_keys_there, clock)
    d_keys = d_keys_all[rows:] + d_keys_there
    d_scale_q = jnp.sum(d_queries * zed, axis=0)
    d_shift_q = jnp.sum(d_queries, axis=0)
    d_scale_k = jnp.sum(d_keys * zed, axis=0)
    d_zpre = as_half((d_queries * scale_q + d_keys * scale_k) * silu_grad(z_pre))
    d_zphi = jnp.concatenate([d_zpre, d_phipre], axis=1)
    grads = [as_half(times_left(mixed_low, d_zphi)), as_half(times_left(mixed_low, d_hpre))]
    sum_wide = Flight(whole_sum, grads, clock)
    clock = sum_v.advance(sum_wide.beside)
    clock = sum_u.advance(clock)
    clock = sum_up.advance(clock)
    keep_up = Flight(kept_rows, [share_of("up", sum_up.finish())], clock)
    clock = sum_g.advance(keep_up.beside)
    clock = sum_wide.advance(clock)
    d_zphi, clock = tied(d_zphi, clock)
    d_mixed = (
        times_right(d_zphi, zphi_full)
        + times_right(d_hpre, full["h"])
        + times_plain(d_gampre, full["g"])
    )
    d_mixed, clock = tied(d_mixed, clock)
    clock = sum_v.advance(clock)
    clock = sum_g.advance(clock)
    clock = sum_wide.advance(clock)
    keep_near = Flight(
        kept_rows, [share_of("u", sum_u.finish()), share_of("g", sum_g.finish())], clock
    )
    clock = keep_down.advance(keep_near.beside)
    clock = keep_up.advance(clock)
    (block["down"],), (block["up"],) = keep_down.finish(), keep_up.finish()
    column_one = Flight(
        lambda x: column_rows(("down", "up"), x), [block["down"], block["up"]], clock
    )
    clock = sum_v.advance(column_one.beside)
    keep_v = Flight(kept_rows, [share_of("v", sum_v.finish())], clock)
    d_mixed, clock = tied(d_mixed, keep_v.beside)
    d_ema = d_mixed * silu_grad(mix_pre)
    d_ema_tiled = tiled(d_ema)
    state_shape = f32_shape(NE, SUBS, LANES)
    first, d_mix, d_state, state_tail = local_call(
        ema_sums_kernel,
        (state_shape,) * 4,
        10 * rows * NE * D,
        8 * rows * D,
        normed_tiled,
        d_ema_tiled,
        decay_tiled,
        start,
    )
    first, clock = tied(first, clock)
    clock = sum_wide.advance(clock)
    clock = column_one.advance(clock)
    behind = carried(first, decay_all, False)
    clock = keep_near.advance(clock)
    block["u"], block["g"] = keep_near.finish()
    clock = sum_wide.advance(clock)
    share_wide = sum_wide.finish()
    keep_wide = Flight(
        kept_rows,
        [
            share_of("phi", share_wide[:, Z : Z + D]),
            share_of("h", share_wide[:, Z + D :]),
            share_of("z", share_wide[:, :Z]),
        ],
        clock,
    )
    clock = keep_v.advance(keep_wide.beside)
    (block["v"],) = keep_v.finish()
    behind, clock = tied(behind, clock)
    d_normed_ema = flat(
        local_call(
            ema_back_kernel,
            f32_shape(rows, SUBS, LANES),
            4 * rows * NE * D,
            8 * rows * D,
            d_ema_tiled,
            decay_tiled,
            mix_tiled,
            behind,
        )
    )
    d_normed_ema, clock = tied(d_normed_ema, clock)
    clock = column_one.advance(clock)
    clock = keep_wide.advance(clock)
    block["phi"], block["h"], block["z"] = keep_wide.finish()
    column_two = Flight(lambda x: column_rows(("u", "g"), x), [block["u"], block["g"]], clock)
    column_three = Flight(
        lambda x: column_rows(("phi", "h", "z"), x),
        [block["phi"], block["h"], block["z"]],
        column_two.beside,
    )
    column_four = Flight(lambda x: column_rows(("v",), x), [block["v"]], column_three.beside)
    columns_held = [item.finish() for item in (column_one, column_two, column_three, column_four)]
    momentum = {name: block[name].astype(jnp.float32) for name in order}
    which = jnp.zeros((), jnp.int32)
    for index, names in enumerate(
        (("down", "up"), ("u", "g"), ("phi", "h", "z"), ("v",))
    ):
        for name in names:
            which = jnp.where(dp_index == SLOT[name], index, which)
    gram = lax.switch(
        which, [lambda *items, i=i: times_left(items[i], items[i]) for i in range(4)], *columns_held
    )
    factor_high, factor_low = orthogonal_factor(gram)
    height = max(block[name].shape[0] for name in order)
    item = chosen(order, [block[name] for name in order], height)
    direction = as_half(times_plain(item, factor_high) + times_plain(item, factor_low))
    tall, middle_rows, low_rows = (size // seq_count for size in (FF, V, D))
    there = across(direction, 1)
    even = own_bit(1) == 0
    first_item, second_item = jnp.where(even, direction, there), jnp.where(even, there, direction)
    packed = jnp.where(
        dp_index < 4,
        jnp.concatenate([first_item[:tall], second_item[:low_rows]], axis=0),
        jnp.concatenate(
            [
                first_item[:middle_rows],
                second_item[:middle_rows],
                jnp.zeros((tall + low_rows - 2 * middle_rows, D), jnp.bfloat16),
            ],
            axis=0,
        ),
    )
    packed = pick(packed.reshape(2, -1, D), 0, own_bit(1))
    packed = lax.all_gather(packed, "dp", axis=0, tiled=True).reshape(-1, tall + low_rows, D)
    updated = {}
    for name in order:
        master = masters[name]
        chip, core = SLOT[name] // 2, SLOT[name] % 2
        at = 0 if core == 0 else (tall if chip < 2 else middle_rows)
        piece = packed[chip, at : at + master.shape[0], : master.shape[1]].astype(jnp.float32)
        rate = MATRIX_RATE * math.sqrt(master.shape[0] * seq_count / FAN[name])
        updated[name] = master - rate * piece

    d_normed_ema, direction = tied(d_normed_ema, direction)
    d_normed = d_normed_all[rows:] + d_normed_there.astype(jnp.float32)
    d_mix = flat(d_mix)
    d_decay = mix * flat(d_state + decay_tiled * behind * state_tail)
    d_eta = d_mix * inject_rate * beta
    d_beta = d_mix * eta * inject_rate
    d_inject = d_mix * eta * beta - d_decay * damp
    d_alpha = d_inject * inject_rate * (1.0 - inject_rate)
    d_delta = -d_decay * inject_rate * damp * (1.0 - damp)
    d_omega = jnp.sum(d_ema * normed, axis=0)
    d_input_norm, d_gain_one = norm_back_one(d_normed + d_normed_ema + omega * d_ema)
    tokens_grad = tokens_grad + d_input_norm

    grad_channel = jnp.concatenate(
        [
            d_gain_one[:, None],
            d_gain_two[:, None],
            d_omega[:, None],
            d_alpha.T,
            d_delta.T,
            d_beta.T,
            d_eta.T,
        ],
        axis=1,
    )
    grad_query = jnp.stack([d_scale_q, d_shift_q, d_scale_k], axis=1)
    query_rows = Z // seq_count
    channel_rows = D // seq_count
    grad_query = jnp.pad(
        grad_query.reshape(seq_count, query_rows, 3),
        ((0, 0), (0, channel_rows - query_rows), (0, 0)),
    ).reshape(D, 3)
    small_sum = summed_small(jnp.concatenate([grad_channel, grad_query], axis=1))
    columns = channel_params.shape[1]
    channel_renewed = MOMENTUM * channel_moment + small_sum[:, :columns]
    query_renewed = MOMENTUM * query_moment + small_sum[:query_rows, columns:]
    squares = jnp.concatenate(
        [
            jnp.sum(channel_renewed * channel_renewed, axis=0),
            jnp.sum(query_renewed * query_renewed, axis=0),
        ]
    )[None]
    squares = sum(others_blocks(squares), squares)[0]
    channel_rms = jnp.sqrt(squares[:columns] / D + 1e-06)
    channel_new = channel_params - VECTOR_RATE * channel_renewed / channel_rms
    query_rms = jnp.sqrt(squares[columns:] / Z + 1e-06)
    query_new = query_params - VECTOR_RATE * query_renewed / query_rms
    return (
        block_output,
        tokens_grad,
        *[updated[name] for name in order],
        *[momentum[name] for name in order],
        channel_new,
        channel_renewed,
        query_new,
        query_renewed,
    )


def solution(mesh):
    token_spec = P(("dp", "seq"), None)
    row_spec = P("seq", None)
    return jax.shard_map(
        body,
        mesh=mesh,
        in_specs=(token_spec, token_spec, P("dp")) + (row_spec,) * 20,
        out_specs=(token_spec, token_spec) + (row_spec,) * 20,
        check_vma=False,
    )
```

```python
import math

import jax
import jax.numpy as jnp
from jax import lax
from jax.experimental import pallas as pl
from jax.experimental.pallas import tpu as pltpu
from jax.sharding import PartitionSpec as P

D = 1024
Z = 128
V = 2048
NE = 16
FF = 4096
NS_STEPS = 5
LANES = 128
SUBS = D // LANES

POLY_A = 3.4445
POLY_B = -4.775
POLY_C = 2.0315
MOMENTUM = 0.5
MATRIX_RATE = 0.5
VECTOR_RATE = 0.2

SLOT = {"up": 0, "z": 1, "down": 2, "phi": 3, "g": 4, "h": 5, "u": 6, "v": 7}
NAMES = ("z", "v", "g", "phi", "h", "u", "up", "down")
FAN = {"z": D, "v": D, "g": D, "phi": D, "h": D, "u": V, "up": D, "down": FF}


def as_half(value):
    return value.astype(jnp.bfloat16)


def times_plain(left, right):
    return jnp.dot(left, right, preferred_element_type=jnp.float32)


def times_right(left, right):
    return lax.dot_general(
        left, right, (((1,), (1,)), ((), ())), preferred_element_type=jnp.float32
    )


def times_left(left, right):
    return lax.dot_general(
        left, right, (((0,), (0,)), ((), ())), preferred_element_type=jnp.float32
    )


def silu_grad(value):
    sig = jax.nn.sigmoid(value)
    return sig * (1.0 + value * (1.0 - sig))


def norm_rows(rows, gain):
    center = rows - jnp.mean(rows, axis=-1, keepdims=True)
    spread = jnp.mean(center * center, axis=-1, keepdims=True)
    return center * lax.rsqrt(spread + 1e-05) * gain


def turned(x, distance):
    count = lax.axis_size("seq")
    return lax.ppermute(x, "seq", [(i, (i + distance) % count) for i in range(count)])


def others_blocks(x):
    return [turned(x, k) for k in range(1, lax.axis_size("seq"))]


def in_order(own, others):
    count, mine = lax.axis_size("seq"), lax.axis_index("seq")
    held = jnp.stack([own] + others)
    rows = [
        lax.dynamic_index_in_dim(held, lax.rem(mine - i + count, count), 0, keepdims=False)
        for i in range(count)
    ]
    return jnp.concatenate(rows, axis=0)


def own_slice(block):
    share = block.shape[0] // lax.axis_size("dp")
    return lax.dynamic_slice_in_dim(block, lax.axis_index("dp") * share, share, 0)


def across(x, bit):
    return lax.ppermute(x, "dp", [(i, i ^ bit) for i in range(lax.axis_size("dp"))])


def chip_bits():
    bits = []
    bit = 2
    while bit < lax.axis_size("dp"):
        bits.append(bit)
        bit *= 2
    return bits, bits[::-1]


def own_bit(bit):
    return lax.rem(lax.axis_index("dp") // bit, 2)


def pick(x, axis, index):
    return lax.dynamic_index_in_dim(x, index, axis, keepdims=False)


def add_half(left, right):
    return as_half(left.astype(jnp.float32) + right.astype(jnp.float32))


class Flight:
    def __init__(self, make, given, beside):
        given, beside = lax.optimization_barrier((given, beside))
        self.steps = make(given)
        self.result = None
        sent, self.moving = next(self.steps)
        self.beside, _ = lax.optimization_barrier((beside, sent))

    def advance(self, beside):
        moving, beside = lax.optimization_barrier((self.moving, beside))
        try:
            sent, self.moving = self.steps.send(moving)
        except StopIteration as end:
            self.result = end.value
            return beside
        beside, _ = lax.optimization_barrier((beside, sent))
        return beside

    def finish(self):
        while self.result is None:
            try:
                _, self.moving = self.steps.send(self.moving)
            except StopIteration as end:
                self.result = end.value
        return self.result


def tied(value, beside):
    return lax.optimization_barrier((value, beside))


def near_gather(blocks):
    count = len(blocks)
    slices = blocks
    share = slices[0].shape[0] // 2
    own = jnp.concatenate([item[:share] for item in slices] + [item[share:] for item in slices], axis=0)
    others = yield [own], others_blocks(own)
    held = jnp.stack([own] + others)
    held = held.reshape(held.shape[0], 2, count, share, -1)
    orders = chip_bits()
    parts = [held[:, index][None] for index in range(2)]
    for step in reversed(range(len(orders[0]))):
        there = yield parts, [across(part, order[step]) for part, order in zip(parts, orders)]
        parts = [jnp.concatenate(pair, axis=0) for pair in zip(parts, there)]
    both = jnp.stack(parts)
    (there,) = yield [both], [across(both, 1)]
    both = jnp.stack([both, there])
    return [both[:, :, :, :, i].reshape(-1, both.shape[-1]) for i in range(count)]


def along_pieces(pieces):
    count = pieces.shape[0]
    moving = yield [pieces], [turned(pieces[k], -k) for k in range(1, count)]
    total = pieces[0].astype(jnp.float32)
    for item in moving:
        total = total + item.astype(jnp.float32)
    return total


def near_sum(grad):
    count = lax.axis_size("seq")
    middle = grad.shape[0] // 2
    (there,) = yield [grad], [across(grad[middle:], 1)]
    cut = middle // 2
    orders = chip_bits()
    parts = [
        (grad[:cut], there[:cut]),
        (grad[cut:middle], there[cut:]),
    ]
    for step in range(len(orders[0])):
        keep, send = [], []
        for mine, theirs in parts:
            rows = mine.shape[0] // 2
            send.append(add_half(mine[rows:], theirs[rows:]))
            keep.append(add_half(mine[:rows], theirs[:rows]))
        there = yield send, [across(item, order[step]) for item, order in zip(send, orders)]
        parts = list(zip(keep, there))
    pieces = jnp.concatenate(
        [add_half(mine, theirs).reshape(count, -1, mine.shape[1]) for mine, theirs in parts], axis=1
    )
    return (yield from along_pieces(pieces))


def far_gather(held):
    return lax.all_gather(held, "dp", axis=0, tiled=False).reshape(-1, held.shape[-1])


def far_sum(grad):
    count = lax.axis_size("seq")
    (part,) = yield [grad], [lax.psum_scatter(grad, "dp", scatter_dimension=0, tiled=True)]
    return (yield from along_pieces(part.reshape(count, -1, grad.shape[1])))


def whole_gather(slices):
    count, dp = lax.axis_size("seq"), lax.axis_size("dp")
    orders = chip_bits()
    others = yield slices, [others_blocks(item) for item in slices]
    parts = [in_order(own[None], [item[None] for item in rest]) for own, rest in zip(slices, others)]
    axes = [[], []]
    for step in list(reversed(range(len(orders[0])))) + [None]:
        bits = [1 if step is None else order[step] for order in orders]
        there = yield parts, [across(part, bit) for part, bit in zip(parts, bits)]
        for index, bit in enumerate(bits):
            mine = own_bit(bit) == 0
            ours, theirs = parts[index], there[index]
            parts[index] = jnp.stack([jnp.where(mine, ours, theirs), jnp.where(mine, theirs, ours)])
            axes[index].insert(0, bit)
    full = []
    for part, names in zip(parts, axes):
        bits = len(names)
        wanted = sorted(names, reverse=True)
        part = jnp.transpose(part, [bits] + [names.index(bit) for bit in wanted] + [bits + 1, bits + 2])
        full.append(part.reshape(-1, part.shape[-1]))
    return full


def whole_sum(grads):
    count, dp = lax.axis_size("seq"), lax.axis_size("dp")
    orders = chip_bits()
    mine = own_bit(1)
    parts = [jnp.swapaxes(g.reshape(count, dp // 2, 2, -1, g.shape[1]), 0, 1) for g in grads]
    send = [pick(part, 2, 1 - mine) for part in parts]
    there = yield send, [across(item, 1) for item in send]
    high = sorted(orders[0], reverse=True)
    split = (2,) * len(high)
    parts = [
        (pick(part, 2, mine).reshape(split + item.shape[1:]), item.reshape(split + item.shape[1:]))
        for part, item in zip(parts, there)
    ]
    axes = [list(high), list(high)]
    for step in range(len(high)):
        keep, send, moving = [], [], []
        for (ours, theirs), order, names in zip(parts, orders, axes):
            bit = order[step]
            axis = names.index(bit)
            names.remove(bit)
            here = own_bit(bit)
            send.append(add_half(pick(ours, axis, 1 - here), pick(theirs, axis, 1 - here)))
            keep.append(add_half(pick(ours, axis, here), pick(theirs, axis, here)))
            moving.append(across(send[-1], bit))
        there = yield send, moving
        parts = list(zip(keep, there))
    both = jnp.concatenate([add_half(ours, theirs) for ours, theirs in parts], axis=2)
    seq_index = lax.axis_index("seq")
    pieces = jnp.stack(
        [pick(both, 0, lax.rem(seq_index - k + count, count)) for k in range(count)]
    )
    return (yield from along_pieces(pieces))


def in_columns(block, slots):
    count = lax.axis_size("seq")
    pairs = [(s * count + i, s * count + (i + 1) % count) for s in slots for i in range(count)]
    held = [block]
    for _ in range(count - 1):
        (item,) = yield [held[-1]], [lax.ppermute(held[-1], ("dp", "seq"), pairs)]
        held.append(item)
    return held


def summed_small(x):
    count, mine, dp = lax.axis_size("seq"), lax.axis_index("seq"), lax.axis_size("dp")
    share = x.shape[0] // count
    held = x.reshape(count, share, x.shape[1])
    total = lax.dynamic_index_in_dim(held, mine, 0, keepdims=False)
    for k in range(1, count):
        piece = lax.dynamic_index_in_dim(held, lax.rem(mine + k, count), 0, keepdims=False)
        total = total + turned(piece, k)
    step = 1
    while step < dp:
        total = total + lax.ppermute(total, "dp", [(i, i ^ step) for i in range(dp)])
        step *= 2
    return total


def ema_end_kernel(u_ref, q_ref, end_ref):
    q = [q_ref[j] for j in range(NE)]

    def step(t, state):
        u = u_ref[t]
        return tuple(q[j] * state[j] + u for j in range(NE))

    zero = jnp.zeros((SUBS, LANES), jnp.float32)
    state = lax.fori_loop(0, u_ref.shape[0], step, (zero,) * NE, unroll=8)
    for j in range(NE):
        end_ref[j] = state[j]


def ema_run_kernel(u_ref, q_ref, w_ref, start_ref, e_ref):
    q = [q_ref[j] for j in range(NE)]
    w = [w_ref[j] for j in range(NE)]

    def step(t, state):
        u = u_ref[t]
        state = tuple(q[j] * state[j] + u for j in range(NE))
        terms = [w[j] * state[j] for j in range(NE)]
        while len(terms) > 1:
            terms = [terms[i] + terms[i + 1] for i in range(0, len(terms), 2)]
        e_ref[t] = terms[0]
        return state

    lax.fori_loop(0, u_ref.shape[0], step, tuple(start_ref[j] for j in range(NE)), unroll=4)


def ema_sums_kernel(u_ref, de_ref, q_ref, start_ref, first_ref, dw_ref, dh_ref, tail_ref):
    rows = u_ref.shape[0]
    zero = jnp.zeros((SUBS, LANES), jnp.float32)
    half = NE // 2
    for base in (0, half):
        q = [q_ref[base + j] for j in range(half)]

        def step(t, carry, q=q):
            h, g, dw, dh, r = carry
            u, de, late = u_ref[t], de_ref[t], de_ref[rows - 1 - t]
            g = tuple(q[j] * g[j] + h[j] for j in range(half))
            h = tuple(q[j] * h[j] + u for j in range(half))
            dw = tuple(dw[j] + de * h[j] for j in range(half))
            dh = tuple(dh[j] + de * g[j] for j in range(half))
            r = tuple(q[j] * r[j] + late for j in range(half))
            return (h, g, dw, dh, r)

        blank = (zero,) * half
        start = tuple(start_ref[base + j] for j in range(half))
        _, g, dw, dh, r = lax.fori_loop(0, rows, step, (start, blank, blank, blank, blank), unroll=2)
        for j in range(half):
            dw_ref[base + j] = dw[j]
            dh_ref[base + j] = dh[j]
            tail_ref[base + j] = g[j]
            first_ref[base + j] = r[j]


def ema_back_kernel(de_ref, q_ref, w_ref, start_ref, du_ref):
    rows = de_ref.shape[0]
    q = [q_ref[j] for j in range(NE)]
    w = [w_ref[j] for j in range(NE)]

    def step(s, state):
        t = rows - 1 - s
        de = de_ref[t]
        state = tuple(q[j] * state[j] + de for j in range(NE))
        terms = [w[j] * state[j] for j in range(NE)]
        while len(terms) > 1:
            terms = [terms[i] + terms[i + 1] for i in range(0, len(terms), 2)]
        du_ref[t] = terms[0]
        return state

    lax.fori_loop(0, rows, step, tuple(start_ref[j] for j in range(NE)), unroll=4)


def f32_shape(*dims):
    return jax.ShapeDtypeStruct(dims, jnp.float32)


def local_call(kernel, out_shape, flops, moved, *args):
    return pl.pallas_call(
        kernel,
        out_shape=out_shape,
        compiler_params=pltpu.CompilerParams(vmem_limit_bytes=24 * 1024 * 1024),
        cost_estimate=pl.CostEstimate(flops=flops, bytes_accessed=moved, transcendentals=0),
    )(*args)


def tiled(x):
    return x.reshape(x.shape[:-1] + (SUBS, LANES))


def flat(x):
    return x.reshape(x.shape[:-2] + (D,))


def carried(ends, decay, forward):
    count, mine = lax.axis_size("seq"), lax.axis_index("seq")
    total = jnp.zeros_like(ends)
    factor = jnp.ones_like(decay)
    for k in range(1, count):
        if forward:
            pairs = [(i, i + k) for i in range(count - k)]
        else:
            pairs = [(i + k, i) for i in range(count - k)]
        total = total + factor * lax.ppermute(ends, "seq", pairs)
        factor = factor * decay
    return total


SIDE = 256


def split_half(value):
    high = value.astype(jnp.bfloat16)
    return high, (value - high.astype(jnp.float32)).astype(jnp.bfloat16)


def factor_kernel(gram_ref, high_ref, low_ref, a_ref, p_ref, t_ref, q_ref):
    side = gram_ref.shape[0]
    count = side // SIDE

    def rows_of(i):
        return slice(i * SIDE, (i + 1) * SIDE)

    def put(ref, i, strip, lead=()):
        for part, value in enumerate(split_half(strip)):
            ref[lead + (part, rows_of(i), slice(i * SIDE, side))] = value
        for j in range(i + 1, count):
            block = strip[:, (j - i) * SIDE : (j - i + 1) * SIDE].T
            for part, value in enumerate(split_half(block)):
                ref[lead + (part, rows_of(j), rows_of(i))] = value

    def strip_of(left, right, i):
        lh, ll = left[0, rows_of(i), :], left[1, rows_of(i), :]
        rh, rl = right[0, :, i * SIDE :], right[1, :, i * SIDE :]
        total = jnp.dot(lh, rl, preferred_element_type=jnp.float32)
        total = total + jnp.dot(ll, rh, preferred_element_type=jnp.float32)
        return total + jnp.dot(lh, rh, preferred_element_type=jnp.float32)

    def diagonal(i, width):
        shape = (SIDE, width)
        return lax.broadcasted_iota(jnp.int32, shape, 0) == lax.broadcasted_iota(
            jnp.int32, shape, 1
        )

    trace = jnp.zeros((1, 1), jnp.float32)
    for i in range(count):
        block = gram_ref[rows_of(i), rows_of(i)]
        block = jnp.where(diagonal(i, SIDE), block, 0.0)
        trace = trace + jnp.sum(jnp.sum(block, axis=0, keepdims=True), axis=1, keepdims=True)
    scale = 1.0 / (jnp.sqrt(trace) + 1e-07)
    for i in range(count):
        for part, value in enumerate(split_half(gram_ref[rows_of(i), :] * (scale * scale))):
            a_ref[part, rows_of(i), :] = value

    def step(k, carry):
        for i in range(count):
            width = side - i * SIDE
            now = a_ref[0, rows_of(i), i * SIDE :].astype(jnp.float32)
            now = now + a_ref[1, rows_of(i), i * SIDE :].astype(jnp.float32)
            strip = POLY_B * now + POLY_C * strip_of(a_ref, a_ref, i)
            put(p_ref, i, jnp.where(diagonal(i, width), strip + POLY_A, strip))

        @pl.when(k < NS_STEPS - 1)
        def _():
            for i in range(count):
                put(t_ref, i, strip_of(a_ref, p_ref, i))
            for i in range(count):
                put(a_ref, i, strip_of(t_ref, p_ref, i))

        there = lax.rem(k, 2)

        @pl.when(k == 0)
        def _():
            q_ref[0] = p_ref[...]

        @pl.when(k > 0)
        def _():
            for i in range(count):
                put(q_ref, i, strip_of(q_ref.at[1 - there], p_ref, i), (there,))

        return carry

    lax.fori_loop(0, NS_STEPS, step, 0)
    last = (NS_STEPS - 1) % 2
    for i in range(count):
        value = q_ref[last, 0, rows_of(i), :].astype(jnp.float32)
        value = (value + q_ref[last, 1, rows_of(i), :].astype(jnp.float32)) * scale
        high_ref[rows_of(i), :], low_ref[rows_of(i), :] = split_half(value)


def orthogonal_factor(gram):
    side = gram.shape[0]
    pair = (2, side, side)
    return pl.pallas_call(
        factor_kernel,
        out_shape=(jax.ShapeDtypeStruct(gram.shape, jnp.bfloat16),) * 2,
        scratch_shapes=[
            pltpu.VMEM(pair, jnp.bfloat16),
            pltpu.VMEM(pair, jnp.bfloat16),
            pltpu.VMEM(pair, jnp.bfloat16),
            pltpu.VMEM((2,) + pair, jnp.bfloat16),
        ],
        compiler_params=pltpu.CompilerParams(vmem_limit_bytes=56 * 1024 * 1024),
        cost_estimate=pl.CostEstimate(
            flops=17 * 4 * side**3, bytes_accessed=8 * side * side, transcendentals=0
        ),
    )(gram)


def body(tokens, cotangent, lengths, *rest):
    order = ("z", "v", "g", "phi", "h", "u", "up", "down")
    masters = dict(zip(order, rest[:8]))
    moments = dict(zip(order, rest[8:16]))
    channel_params, channel_moment, query_params, query_moment = rest[16:]
    seq_count = lax.axis_size("seq")
    seq_index = lax.axis_index("seq")
    dp_count = lax.axis_size("dp")
    dp_index = lax.axis_index("dp")
    rows = tokens.shape[0]

    half = {name: as_half(own_slice(masters[name])) for name in order}
    far_own = jnp.concatenate([half["up"], half["down"]], axis=0)
    far_held = jnp.stack([far_own] + others_blocks(far_own))
    cut = half["up"].shape[0]
    full = {"up": far_gather(far_held[:, :cut]), "down": far_gather(far_held[:, cut:])}
    small = jnp.concatenate(
        [
            channel_params,
            jnp.pad(query_params, ((0, channel_params.shape[0] - query_params.shape[0]), (0, 0))),
        ],
        axis=1,
    )
    small = as_half(small)
    small_all = in_order(small, others_blocks(small)).astype(jnp.float32)
    channel = small_all[:, : channel_params.shape[1]]
    query_set = small_all.reshape(seq_count, -1, small_all.shape[1])[
        :, : query_params.shape[0], channel_params.shape[1] :
    ].reshape(Z, 3)
    get_v = Flight(near_gather, [half["v"]], small)

    gain_one = channel[:, 0]
    gain_two = channel[:, 1]
    omega = channel[:, 2]
    alpha, delta, beta, eta = (
        channel[:, 3 + k * NE : 3 + (k + 1) * NE].T for k in range(4)
    )
    scale_q = query_set[:, 0]
    shift_q = query_set[:, 1]
    scale_k = query_set[:, 2]
    score_scale = Z ** (-0.5)

    place = seq_index * rows + jnp.arange(rows, dtype=jnp.int32)
    keep = (place < lengths[0]).astype(jnp.float32)[:, None]
    inputs = tokens.astype(jnp.float32)
    weighted = cotangent.astype(jnp.float32) * keep
    back_ffn = as_half(weighted)
    evens = [(i, i + 1) for i in range(0, seq_count - 1, 2)]
    odds = [(i + 1, i) for i in range(0, seq_count - 1, 2)]

    normed, norm_back_one = jax.vjp(norm_rows, inputs, gain_one)
    normed_low = as_half(normed)
    inject_rate = jax.nn.sigmoid(alpha)
    damp = jax.nn.sigmoid(delta)
    decay = 1.0 - inject_rate * damp
    mix = eta * inject_rate * beta
    decay_tiled, mix_tiled = tiled(decay), tiled(mix)
    decay_all = decay_tiled**rows
    normed_tiled = tiled(normed)
    ends = local_call(
        ema_end_kernel, f32_shape(NE, SUBS, LANES), 2 * rows * NE * D, 4 * rows * D, normed_tiled, decay_tiled
    )
    normed_there = lax.ppermute(normed_low, "seq", evens)
    clock = get_v.advance(ends)
    ends = clock
    zphi_slice = jnp.concatenate([half["z"], half["phi"]], axis=1)
    get_wide = Flight(whole_gather, [zphi_slice, half["h"]], clock)
    clock = get_v.advance(get_wide.beside)
    start = carried(ends, decay_all, True)
    clock = get_wide.advance(clock)
    clock = get_v.advance(clock)
    start, clock = tied(start, clock)
    ema_out = local_call(
        ema_run_kernel,
        f32_shape(rows, SUBS, LANES),
        4 * rows * NE * D,
        8 * rows * D,
        normed_tiled,
        decay_tiled,
        mix_tiled,
        start,
    )
    ema_out, clock = tied(ema_out, clock)
    clock = get_wide.advance(clock)
    clock = get_v.advance(clock)
    (full["v"],) = get_v.finish()
    normed_both = jnp.concatenate([normed_there, normed_low], axis=0)
    normed_both, clock = tied(normed_both, clock)
    v_pre = times_right(normed_both, full["v"])
    values_all = as_half(jax.nn.silu(v_pre))
    values_all, clock = tied(values_all, clock)
    clock = get_wide.advance(clock)
    get_near = Flight(near_gather, [half["g"], half["u"]], clock)
    clock = get_wide.advance(get_near.beside)
    zphi_full, full["h"] = get_wide.finish()
    full["z"], full["phi"] = zphi_full[:, :Z], zphi_full[:, Z:]
    ema_out, clock = tied(ema_out, clock)
    mix_pre = flat(ema_out) + omega * normed
    mixed_low = as_half(jax.nn.silu(mix_pre))
    z_pre = times_plain(mixed_low, full["z"])
    zed = jax.nn.silu(z_pre)
    queries_low = as_half(zed * scale_q + shift_q)
    keys_low = as_half(zed * scale_k)
    keys_there = lax.ppermute(keys_low, "seq", evens)
    phi = jax.nn.sigmoid(times_plain(mixed_low, full["phi"]))
    h_part = times_plain(mixed_low, full["h"])
    keys_there, h_part, clock = lax.optimization_barrier((keys_there, h_part, clock))
    clock = get_near.advance(clock)
    keys_all = jnp.concatenate([keys_there, keys_low], axis=0)
    odd_device = seq_index % 2 == 1
    query_place = jnp.arange(rows)[:, None]
    key_place = jnp.arange(2 * rows)[None, :]
    allowed = jnp.where(key_place < rows, odd_device, key_place - rows <= query_place)
    queries_low, clock = tied(queries_low, clock)
    scores = jnp.where(allowed, times_right(queries_low, keys_all) * score_scale, -1e30)
    top = jnp.max(scores, axis=-1, keepdims=True)
    expo = jnp.exp(scores - top)
    probs = expo / jnp.sum(expo, axis=-1, keepdims=True)
    probs_low = as_half(probs)
    attended = times_plain(probs_low, values_all)
    attended, clock = tied(attended, clock)
    clock = get_near.advance(clock)
    clock = get_near.advance(clock)
    clock = get_near.advance(clock)
    full["g"], full["u"] = get_near.finish()
    mixed_low, clock = tied(mixed_low, clock)
    gam_pre = times_right(mixed_low, full["g"])
    gamma = jax.nn.silu(gam_pre)
    gated_low = as_half(gamma * attended)
    h_pre = h_part + times_plain(gated_low, full["u"])
    cand = jax.nn.silu(h_pre)
    middle = phi * cand + (1.0 - phi) * inputs
    wide, norm_back_two = jax.vjp(norm_rows, middle, gain_two)
    wide_low = as_half(wide)
    a_pre = times_right(wide_low, full["up"])
    active_low = as_half(jax.nn.silu(a_pre))
    result = middle + times_plain(active_low, full["down"])
    block_output = as_half(result * keep)

    def share_of(name, total):
        return as_half(MOMENTUM * own_slice(moments[name]) + total)

    def kept_rows(shares):
        packed = jnp.concatenate([item.reshape(-1, D) for item in shares], axis=0)
        (packed,) = yield [packed], [lax.all_gather(packed, "dp", axis=0, tiled=False)]
        out, at = [], 0
        for item in shares:
            size = item.size // D
            out.append(packed[:, at : at + size].reshape(-1, item.shape[1]))
            at += size
        return out

    def column_rows(names, blocks):
        height = max(item.shape[0] for item in blocks)
        own = chosen(names, blocks, height)
        held = yield from in_columns(own, [SLOT[name] for name in names])
        return held

    def chosen(names, blocks, height):
        out = jnp.zeros((height, D), jnp.bfloat16)
        for name, item in zip(names, blocks):
            item = jnp.pad(item, ((0, height - item.shape[0]), (0, D - item.shape[1])))
            out = jnp.where(dp_index == SLOT[name], item, out)
        return out

    block = {}
    orders = chip_bits()

    clock = result
    grad = as_half(times_left(active_low, back_ffn))
    sum_down = Flight(far_sum, grad, clock)
    back_ffn, clock = tied(back_ffn, sum_down.beside)
    d_apre = as_half(times_right(back_ffn, full["down"]) * silu_grad(a_pre))
    d_apre, clock = tied(d_apre, clock)
    grad = as_half(times_left(d_apre, wide_low))
    sum_up = Flight(far_sum, grad, clock)
    clock = sum_up.beside
    d_apre, clock = tied(d_apre, clock)
    d_mid_norm, d_gain_two = norm_back_two(times_plain(d_apre, full["up"]))
    d_middle = weighted + d_mid_norm
    d_phipre = as_half(d_middle * (cand - inputs) * phi * (1.0 - phi))
    d_hpre = as_half(d_middle * phi * silu_grad(h_pre))
    tokens_grad = d_middle * (1.0 - phi)
    d_hpre, clock = tied(d_hpre, clock)
    grad = as_half(times_left(gated_low, d_hpre))
    sum_u = Flight(near_sum, grad, clock)
    d_hpre, clock = tied(d_hpre, sum_u.beside)
    d_gated = times_right(d_hpre, full["u"])
    d_attended = as_half(d_gated * gamma)
    d_gampre = as_half(d_gated * attended * silu_grad(gam_pre))
    d_gampre, clock = tied(d_gampre, clock)
    clock = sum_u.advance(clock)
    d_gampre, clock = tied(d_gampre, clock)
    grad = as_half(times_left(d_gampre, mixed_low))
    sum_g = Flight(near_sum, grad, clock)
    d_attended, clock = tied(d_attended, sum_g.beside)
    d_probs = times_right(d_attended, values_all)
    d_scores = as_half(probs * (d_probs - jnp.sum(probs * d_probs, axis=-1, keepdims=True)))
    d_scores, clock = tied(d_scores, clock)
    clock = sum_g.advance(clock)
    d_attended, clock = tied(d_attended, clock)
    d_vpre = as_half(times_left(probs_low, d_attended) * silu_grad(v_pre))
    d_vpre, clock = tied(d_vpre, clock)
    clock = sum_down.advance(clock)
    clock = sum_u.advance(clock)
    d_vpre, clock = tied(d_vpre, clock)
    grad = as_half(times_left(d_vpre, normed_both))
    sum_v = Flight(near_sum, grad, clock)
    d_vpre, clock = tied(d_vpre, sum_v.beside)
    d_queries = times_plain(d_scores, keys_all) * score_scale
    d_keys_all = times_left(d_scores, queries_low) * score_scale
    d_keys_there = lax.ppermute(d_keys_all[:rows], "seq", odds)
    d_normed_all = times_plain(d_vpre, full["v"])
    d_normed_there = lax.ppermute(as_half(d_normed_all[:rows]), "seq", odds)
    d_normed_all, clock = tied(d_normed_all, clock)
    clock = sum_v.advance(clock)
    clock = sum_g.advance(clock)
    clock = sum_down.advance(clock)
    keep_down = Flight(kept_rows, [share_of("down", sum_down.finish())], clock)
    clock = sum_up.advance(keep_down.beside)
    d_keys_there, clock = tied(d_keys_there, clock)
    d_keys = d_keys_all[rows:] + d_keys_there
    d_scale_q = jnp.sum(d_queries * zed, axis=0)
    d_shift_q = jnp.sum(d_queries, axis=0)
    d_scale_k = jnp.sum(d_keys * zed, axis=0)
    d_zpre = as_half((d_queries * scale_q + d_keys * scale_k) * silu_grad(z_pre))
    d_zphi = jnp.concatenate([d_zpre, d_phipre], axis=1)
    grads = [as_half(times_left(mixed_low, d_zphi)), as_half(times_left(mixed_low, d_hpre))]
    sum_wide = Flight(whole_sum, grads, clock)
    clock = sum_v.advance(sum_wide.beside)
    clock = sum_u.advance(clock)
    clock = sum_up.advance(clock)
    keep_up = Flight(kept_rows, [share_of("up", sum_up.finish())], clock)
    clock = sum_g.advance(keep_up.beside)
    clock = sum_wide.advance(clock)
    d_zphi, clock = tied(d_zphi, clock)
    d_mixed = (
        times_right(d_zphi, zphi_full)
        + times_right(d_hpre, full["h"])
        + times_plain(d_gampre, full["g"])
    )
    d_mixed, clock = tied(d_mixed, clock)
    clock = sum_v.advance(clock)
    clock = sum_g.advance(clock)
    clock = sum_wide.advance(clock)
    keep_near = Flight(
        kept_rows, [share_of("u", sum_u.finish()), share_of("g", sum_g.finish())], clock
    )
    clock = keep_down.advance(keep_near.beside)
    clock = keep_up.advance(clock)
    (block["down"],), (block["up"],) = keep_down.finish(), keep_up.finish()
    column_one = Flight(
        lambda x: column_rows(("down", "up"), x), [block["down"], block["up"]], clock
    )
    clock = sum_v.advance(column_one.beside)
    keep_v = Flight(kept_rows, [share_of("v", sum_v.finish())], clock)
    d_mixed, clock = tied(d_mixed, keep_v.beside)
    d_ema = d_mixed * silu_grad(mix_pre)
    d_ema_tiled = tiled(d_ema)
    state_shape = f32_shape(NE, SUBS, LANES)
    first, d_mix, d_state, state_tail = local_call(
        ema_sums_kernel,
        (state_shape,) * 4,
        10 * rows * NE * D,
        8 * rows * D,
        normed_tiled,
        d_ema_tiled,
        decay_tiled,
        start,
    )
    first, clock = tied(first, clock)
    clock = sum_wide.advance(clock)
    clock = column_one.advance(clock)
    behind = carried(first, decay_all, False)
    clock = keep_near.advance(clock)
    block["u"], block["g"] = keep_near.finish()
    clock = sum_wide.advance(clock)
    share_wide = sum_wide.finish()
    keep_wide = Flight(
        kept_rows,
        [
            share_of("phi", share_wide[:, Z : Z + D]),
            share_of("h", share_wide[:, Z + D :]),
            share_of("z", share_wide[:, :Z]),
        ],
        clock,
    )
    clock = keep_v.advance(keep_wide.beside)
    (block["v"],) = keep_v.finish()
    behind, clock = tied(behind, clock)
    d_normed_ema = flat(
        local_call(
            ema_back_kernel,
            f32_shape(rows, SUBS, LANES),
            4 * rows * NE * D,
            8 * rows * D,
            d_ema_tiled,
            decay_tiled,
            mix_tiled,
            behind,
        )
    )
    d_normed_ema, clock = tied(d_normed_ema, clock)
    clock = column_one.advance(clock)
    clock = keep_wide.advance(clock)
    block["phi"], block["h"], block["z"] = keep_wide.finish()
    column_two = Flight(lambda x: column_rows(("u", "g"), x), [block["u"], block["g"]], clock)
    column_three = Flight(
        lambda x: column_rows(("phi", "h", "z"), x),
        [block["phi"], block["h"], block["z"]],
        column_two.beside,
    )
    column_four = Flight(lambda x: column_rows(("v",), x), [block["v"]], column_three.beside)
    columns_held = [item.finish() for item in (column_one, column_two, column_three, column_four)]
    momentum = {name: block[name].astype(jnp.float32) for name in order}
    which = jnp.zeros((), jnp.int32)
    for index, names in enumerate(
        (("down", "up"), ("u", "g"), ("phi", "h", "z"), ("v",))
    ):
        for name in names:
            which = jnp.where(dp_index == SLOT[name], index, which)
    def gram_of(items):
        whole = jnp.concatenate(items, axis=0)
        return times_left(whole, whole)

    gram = lax.switch(
        which, [lambda *items, i=i: gram_of(items[i]) for i in range(4)], *columns_held
    )
    factor_high, factor_low = orthogonal_factor(gram)
    height = max(block[name].shape[0] for name in order)
    item = chosen(order, [block[name] for name in order], height)
    direction = as_half(times_plain(item, factor_high) + times_plain(item, factor_low))
    tall, middle_rows, low_rows = (size // seq_count for size in (FF, V, D))
    there = across(direction, 1)
    even = own_bit(1) == 0
    first_item, second_item = jnp.where(even, direction, there), jnp.where(even, there, direction)
    packed = jnp.where(
        dp_index < 4,
        jnp.concatenate([first_item[:tall], second_item[:low_rows]], axis=0),
        jnp.concatenate(
            [
                first_item[:middle_rows],
                second_item[:middle_rows],
                jnp.zeros((tall + low_rows - 2 * middle_rows, D), jnp.bfloat16),
            ],
            axis=0,
        ),
    )
    packed = pick(packed.reshape(2, -1, D), 0, own_bit(1))
    packed = lax.all_gather(packed, "dp", axis=0, tiled=True).reshape(-1, tall + low_rows, D)
    updated = {}
    for name in order:
        master = masters[name]
        chip, core = SLOT[name] // 2, SLOT[name] % 2
        at = 0 if core == 0 else (tall if chip < 2 else middle_rows)
        piece = packed[chip, at : at + master.shape[0], : master.shape[1]].astype(jnp.float32)
        rate = MATRIX_RATE * math.sqrt(master.shape[0] * seq_count / FAN[name])
        updated[name] = master - rate * piece

    d_normed_ema, direction = tied(d_normed_ema, direction)
    d_normed = d_normed_all[rows:] + d_normed_there.astype(jnp.float32)
    d_mix = flat(d_mix)
    d_decay = mix * flat(d_state + decay_tiled * behind * state_tail)
    d_eta = d_mix * inject_rate * beta
    d_beta = d_mix * eta * inject_rate
    d_inject = d_mix * eta * beta - d_decay * damp
    d_alpha = d_inject * inject_rate * (1.0 - inject_rate)
    d_delta = -d_decay * inject_rate * damp * (1.0 - damp)
    d_omega = jnp.sum(d_ema * normed, axis=0)
    d_input_norm, d_gain_one = norm_back_one(d_normed + d_normed_ema + omega * d_ema)
    tokens_grad = tokens_grad + d_input_norm

    grad_channel = jnp.concatenate(
        [
            d_gain_one[:, None],
            d_gain_two[:, None],
            d_omega[:, None],
            d_alpha.T,
            d_delta.T,
            d_beta.T,
            d_eta.T,
        ],
        axis=1,
    )
    grad_query = jnp.stack([d_scale_q, d_shift_q, d_scale_k], axis=1)
    query_rows = Z // seq_count
    channel_rows = D // seq_count
    grad_query = jnp.pad(
        grad_query.reshape(seq_count, query_rows, 3),
        ((0, 0), (0, channel_rows - query_rows), (0, 0)),
    ).reshape(D, 3)
    small_sum = summed_small(jnp.concatenate([grad_channel, grad_query], axis=1))
    columns = channel_params.shape[1]
    channel_renewed = MOMENTUM * channel_moment + small_sum[:, :columns]
    query_renewed = MOMENTUM * query_moment + small_sum[:query_rows, columns:]
    squares = jnp.concatenate(
        [
            jnp.sum(channel_renewed * channel_renewed, axis=0),
            jnp.sum(query_renewed * query_renewed, axis=0),
        ]
    )[None]
    squares = sum(others_blocks(squares), squares)[0]
    channel_rms = jnp.sqrt(squares[:columns] / D + 1e-06)
    channel_new = channel_params - VECTOR_RATE * channel_renewed / channel_rms
    query_rms = jnp.sqrt(squares[columns:] / Z + 1e-06)
    query_new = query_params - VECTOR_RATE * query_renewed / query_rms
    return (
        block_output,
        tokens_grad,
        *[updated[name] for name in order],
        *[momentum[name] for name in order],
        channel_new,
        channel_renewed,
        query_new,
        query_renewed,
    )


def solution(mesh):
    token_spec = P(("dp", "seq"), None)
    row_spec = P("seq", None)
    return jax.shard_map(
        body,
        mesh=mesh,
        in_specs=(token_spec, token_spec, P("dp")) + (row_spec,) * 20,
        out_specs=(token_spec, token_spec) + (row_spec,) * 20,
        check_vma=False,
    )
```

```python
import math

import jax
import jax.numpy as jnp
from jax import lax
from jax.experimental import pallas as pl
from jax.experimental.pallas import tpu as pltpu
from jax.sharding import PartitionSpec as P

D = 1024
Z = 128
V = 2048
NE = 16
FF = 4096
NS_STEPS = 5
LANES = 128
SUBS = D // LANES

POLY_A = 3.4445
POLY_B = -4.775
POLY_C = 2.0315
MOMENTUM = 0.5
MATRIX_RATE = 0.5
VECTOR_RATE = 0.2

SLOT = {"up": 0, "z": 1, "down": 2, "phi": 3, "g": 4, "h": 5, "u": 6, "v": 7}
NAMES = ("z", "v", "g", "phi", "h", "u", "up", "down")
FAN = {"z": D, "v": D, "g": D, "phi": D, "h": D, "u": V, "up": D, "down": FF}


def as_half(value):
    return value.astype(jnp.bfloat16)


def times_plain(left, right):
    return jnp.dot(left, right, preferred_element_type=jnp.float32)


def times_right(left, right):
    return lax.dot_general(
        left, right, (((1,), (1,)), ((), ())), preferred_element_type=jnp.float32
    )


def times_left(left, right):
    return lax.dot_general(
        left, right, (((0,), (0,)), ((), ())), preferred_element_type=jnp.float32
    )


def silu_grad(value):
    sig = jax.nn.sigmoid(value)
    return sig * (1.0 + value * (1.0 - sig))


def norm_rows(rows, gain):
    center = rows - jnp.mean(rows, axis=-1, keepdims=True)
    spread = jnp.mean(center * center, axis=-1, keepdims=True)
    return center * lax.rsqrt(spread + 1e-05) * gain


def turned(x, distance):
    count = lax.axis_size("seq")
    return lax.ppermute(x, "seq", [(i, (i + distance) % count) for i in range(count)])


def others_blocks(x):
    return [turned(x, k) for k in range(1, lax.axis_size("seq"))]


def in_order(own, others):
    count, mine = lax.axis_size("seq"), lax.axis_index("seq")
    held = jnp.stack([own] + others)
    rows = [
        lax.dynamic_index_in_dim(held, lax.rem(mine - i + count, count), 0, keepdims=False)
        for i in range(count)
    ]
    return jnp.concatenate(rows, axis=0)


def own_slice(block):
    share = block.shape[0] // lax.axis_size("dp")
    return lax.dynamic_slice_in_dim(block, lax.axis_index("dp") * share, share, 0)


def across(x, bit):
    return lax.ppermute(x, "dp", [(i, i ^ bit) for i in range(lax.axis_size("dp"))])


def chip_bits():
    bits = []
    bit = 2
    while bit < lax.axis_size("dp"):
        bits.append(bit)
        bit *= 2
    return bits, bits[::-1]


def own_bit(bit):
    return lax.rem(lax.axis_index("dp") // bit, 2)


def pick(x, axis, index):
    return lax.dynamic_index_in_dim(x, index, axis, keepdims=False)


def add_half(left, right):
    return as_half(left.astype(jnp.float32) + right.astype(jnp.float32))


class Flight:
    def __init__(self, make, given, beside):
        given, beside = lax.optimization_barrier((given, beside))
        self.steps = make(given)
        self.result = None
        sent, self.moving = next(self.steps)
        self.beside, _ = lax.optimization_barrier((beside, sent))

    def advance(self, beside):
        moving, beside = lax.optimization_barrier((self.moving, beside))
        try:
            sent, self.moving = self.steps.send(moving)
        except StopIteration as end:
            self.result = end.value
            return beside
        beside, _ = lax.optimization_barrier((beside, sent))
        return beside

    def finish(self):
        while self.result is None:
            try:
                _, self.moving = self.steps.send(self.moving)
            except StopIteration as end:
                self.result = end.value
        return self.result


def tied(value, beside):
    return lax.optimization_barrier((value, beside))


def near_gather(blocks):
    count = len(blocks)
    slices = blocks
    share = slices[0].shape[0] // 2
    own = jnp.concatenate([item[:share] for item in slices] + [item[share:] for item in slices], axis=0)
    others = yield [own], others_blocks(own)
    held = jnp.stack([own] + others)
    held = held.reshape(held.shape[0], 2, count, share, -1)
    orders = chip_bits()
    parts = [held[:, index][None] for index in range(2)]
    for step in reversed(range(len(orders[0]))):
        there = yield parts, [across(part, order[step]) for part, order in zip(parts, orders)]
        parts = [jnp.concatenate(pair, axis=0) for pair in zip(parts, there)]
    both = jnp.stack(parts)
    (there,) = yield [both], [across(both, 1)]
    both = jnp.stack([both, there])
    return [both[:, :, :, :, i].reshape(-1, both.shape[-1]) for i in range(count)]


def along_pieces(pieces):
    count = pieces.shape[0]
    moving = yield [pieces], [turned(pieces[k], -k) for k in range(1, count)]
    total = pieces[0].astype(jnp.float32)
    for item in moving:
        total = total + item.astype(jnp.float32)
    return total


def near_sum(grad):
    count = lax.axis_size("seq")
    middle = grad.shape[0] // 2
    (there,) = yield [grad], [across(grad[middle:], 1)]
    cut = middle // 2
    orders = chip_bits()
    parts = [
        (grad[:cut], there[:cut]),
        (grad[cut:middle], there[cut:]),
    ]
    for step in range(len(orders[0])):
        keep, send = [], []
        for mine, theirs in parts:
            rows = mine.shape[0] // 2
            send.append(add_half(mine[rows:], theirs[rows:]))
            keep.append(add_half(mine[:rows], theirs[:rows]))
        there = yield send, [across(item, order[step]) for item, order in zip(send, orders)]
        parts = list(zip(keep, there))
    pieces = jnp.concatenate(
        [add_half(mine, theirs).reshape(count, -1, mine.shape[1]) for mine, theirs in parts], axis=1
    )
    return (yield from along_pieces(pieces))


def far_gather(held):
    return lax.all_gather(held, "dp", axis=0, tiled=False).reshape(-1, held.shape[-1])


def far_sum(grad):
    count = lax.axis_size("seq")
    (part,) = yield [grad], [lax.psum_scatter(grad, "dp", scatter_dimension=0, tiled=True)]
    return (yield from along_pieces(part.reshape(count, -1, grad.shape[1])))


def whole_gather(slices):
    count, dp = lax.axis_size("seq"), lax.axis_size("dp")
    orders = chip_bits()
    others = yield slices, [others_blocks(item) for item in slices]
    parts = [in_order(own[None], [item[None] for item in rest]) for own, rest in zip(slices, others)]
    axes = [[], []]
    for step in list(reversed(range(len(orders[0])))) + [None]:
        bits = [1 if step is None else order[step] for order in orders]
        there = yield parts, [across(part, bit) for part, bit in zip(parts, bits)]
        for index, bit in enumerate(bits):
            mine = own_bit(bit) == 0
            ours, theirs = parts[index], there[index]
            parts[index] = jnp.stack([jnp.where(mine, ours, theirs), jnp.where(mine, theirs, ours)])
            axes[index].insert(0, bit)
    full = []
    for part, names in zip(parts, axes):
        bits = len(names)
        wanted = sorted(names, reverse=True)
        part = jnp.transpose(part, [bits] + [names.index(bit) for bit in wanted] + [bits + 1, bits + 2])
        full.append(part.reshape(-1, part.shape[-1]))
    return full


def whole_sum(grads):
    count, dp = lax.axis_size("seq"), lax.axis_size("dp")
    orders = chip_bits()
    mine = own_bit(1)
    parts = [jnp.swapaxes(g.reshape(count, dp // 2, 2, -1, g.shape[1]), 0, 1) for g in grads]
    send = [pick(part, 2, 1 - mine) for part in parts]
    there = yield send, [across(item, 1) for item in send]
    high = sorted(orders[0], reverse=True)
    split = (2,) * len(high)
    parts = [
        (pick(part, 2, mine).reshape(split + item.shape[1:]), item.reshape(split + item.shape[1:]))
        for part, item in zip(parts, there)
    ]
    axes = [list(high), list(high)]
    for step in range(len(high)):
        keep, send, moving = [], [], []
        for (ours, theirs), order, names in zip(parts, orders, axes):
            bit = order[step]
            axis = names.index(bit)
            names.remove(bit)
            here = own_bit(bit)
            send.append(add_half(pick(ours, axis, 1 - here), pick(theirs, axis, 1 - here)))
            keep.append(add_half(pick(ours, axis, here), pick(theirs, axis, here)))
            moving.append(across(send[-1], bit))
        there = yield send, moving
        parts = list(zip(keep, there))
    both = jnp.concatenate([add_half(ours, theirs) for ours, theirs in parts], axis=2)
    seq_index = lax.axis_index("seq")
    pieces = jnp.stack(
        [pick(both, 0, lax.rem(seq_index - k + count, count)) for k in range(count)]
    )
    return (yield from along_pieces(pieces))


def in_columns(block, slots):
    count = lax.axis_size("seq")
    pairs = [(s * count + i, s * count + (i + 1) % count) for s in slots for i in range(count)]
    held = [block]
    for _ in range(count - 1):
        (item,) = yield [held[-1]], [lax.ppermute(held[-1], ("dp", "seq"), pairs)]
        held.append(item)
    return held


def summed_small(x):
    count, mine, dp = lax.axis_size("seq"), lax.axis_index("seq"), lax.axis_size("dp")
    share = x.shape[1] // count
    total = lax.dynamic_slice_in_dim(x, mine * share, share, 1)
    for k in range(1, count):
        there = lax.rem(mine + k, count)
        total = total + turned(lax.dynamic_slice_in_dim(x, there * share, share, 1), k)
    step = 1
    while step < dp:
        total = total + lax.ppermute(total, "dp", [(i, i ^ step) for i in range(dp)])
        step *= 2
    return total


def ema_end_kernel(u_ref, q_ref, end_ref):
    q = [q_ref[j] for j in range(NE)]

    def step(t, state):
        u = u_ref[t]
        return tuple(q[j] * state[j] + u for j in range(NE))

    zero = jnp.zeros((SUBS, LANES), jnp.float32)
    state = lax.fori_loop(0, u_ref.shape[0], step, (zero,) * NE, unroll=8)
    for j in range(NE):
        end_ref[j] = state[j]


def ema_run_kernel(u_ref, q_ref, w_ref, start_ref, e_ref):
    q = [q_ref[j] for j in range(NE)]
    w = [w_ref[j] for j in range(NE)]

    def step(t, state):
        u = u_ref[t]
        state = tuple(q[j] * state[j] + u for j in range(NE))
        terms = [w[j] * state[j] for j in range(NE)]
        while len(terms) > 1:
            terms = [terms[i] + terms[i + 1] for i in range(0, len(terms), 2)]
        e_ref[t] = terms[0]
        return state

    lax.fori_loop(0, u_ref.shape[0], step, tuple(start_ref[j] for j in range(NE)), unroll=4)


def ema_sums_kernel(u_ref, de_ref, q_ref, start_ref, first_ref, dw_ref, dh_ref, tail_ref):
    rows = u_ref.shape[0]
    zero = jnp.zeros((SUBS, LANES), jnp.float32)
    half = NE // 2
    for base in (0, half):
        q = [q_ref[base + j] for j in range(half)]

        def step(t, carry, q=q):
            h, g, dw, dh, r = carry
            u, de, late = u_ref[t], de_ref[t], de_ref[rows - 1 - t]
            g = tuple(q[j] * g[j] + h[j] for j in range(half))
            h = tuple(q[j] * h[j] + u for j in range(half))
            dw = tuple(dw[j] + de * h[j] for j in range(half))
            dh = tuple(dh[j] + de * g[j] for j in range(half))
            r = tuple(q[j] * r[j] + late for j in range(half))
            return (h, g, dw, dh, r)

        blank = (zero,) * half
        start = tuple(start_ref[base + j] for j in range(half))
        _, g, dw, dh, r = lax.fori_loop(0, rows, step, (start, blank, blank, blank, blank), unroll=2)
        for j in range(half):
            dw_ref[base + j] = dw[j]
            dh_ref[base + j] = dh[j]
            tail_ref[base + j] = g[j]
            first_ref[base + j] = r[j]


def ema_back_kernel(de_ref, q_ref, w_ref, start_ref, du_ref):
    rows = de_ref.shape[0]
    q = [q_ref[j] for j in range(NE)]
    w = [w_ref[j] for j in range(NE)]

    def step(s, state):
        t = rows - 1 - s
        de = de_ref[t]
        state = tuple(q[j] * state[j] + de for j in range(NE))
        terms = [w[j] * state[j] for j in range(NE)]
        while len(terms) > 1:
            terms = [terms[i] + terms[i + 1] for i in range(0, len(terms), 2)]
        du_ref[t] = terms[0]
        return state

    lax.fori_loop(0, rows, step, tuple(start_ref[j] for j in range(NE)), unroll=4)


def f32_shape(*dims):
    return jax.ShapeDtypeStruct(dims, jnp.float32)


def local_call(kernel, out_shape, flops, moved, *args):
    return pl.pallas_call(
        kernel,
        out_shape=out_shape,
        compiler_params=pltpu.CompilerParams(vmem_limit_bytes=24 * 1024 * 1024),
        cost_estimate=pl.CostEstimate(flops=flops, bytes_accessed=moved, transcendentals=0),
    )(*args)


def tiled(x):
    return x.reshape(x.shape[:-1] + (SUBS, LANES))


def flat(x):
    return x.reshape(x.shape[:-2] + (D,))


def carried(ends, decay, forward):
    count, mine = lax.axis_size("seq"), lax.axis_index("seq")
    total = jnp.zeros_like(ends)
    factor = jnp.ones_like(decay)
    for k in range(1, count):
        if forward:
            pairs = [(i, i + k) for i in range(count - k)]
        else:
            pairs = [(i + k, i) for i in range(count - k)]
        total = total + factor * lax.ppermute(ends, "seq", pairs)
        factor = factor * decay
    return total


SIDE = 256


def split_half(value):
    high = value.astype(jnp.bfloat16)
    return high, (value - high.astype(jnp.float32)).astype(jnp.bfloat16)


def factor_kernel(gram_ref, high_ref, low_ref, a_ref, p_ref, t_ref, q_ref):
    side = gram_ref.shape[0]
    count = side // SIDE

    def rows_of(i):
        return slice(i * SIDE, (i + 1) * SIDE)

    def put(ref, i, strip, lead=()):
        for part, value in enumerate(split_half(strip)):
            ref[lead + (part, rows_of(i), slice(i * SIDE, side))] = value
        for j in range(i + 1, count):
            block = strip[:, (j - i) * SIDE : (j - i + 1) * SIDE].T
            for part, value in enumerate(split_half(block)):
                ref[lead + (part, rows_of(j), rows_of(i))] = value

    def strip_of(left, right, i):
        lh, ll = left[0, rows_of(i), :], left[1, rows_of(i), :]
        rh, rl = right[0, :, i * SIDE :], right[1, :, i * SIDE :]
        total = jnp.dot(lh, rl, preferred_element_type=jnp.float32)
        total = total + jnp.dot(ll, rh, preferred_element_type=jnp.float32)
        return total + jnp.dot(lh, rh, preferred_element_type=jnp.float32)

    def diagonal(i, width):
        shape = (SIDE, width)
        return lax.broadcasted_iota(jnp.int32, shape, 0) == lax.broadcasted_iota(
            jnp.int32, shape, 1
        )

    trace = jnp.zeros((1, 1), jnp.float32)
    for i in range(count):
        block = gram_ref[rows_of(i), rows_of(i)]
        block = jnp.where(diagonal(i, SIDE), block, 0.0)
        trace = trace + jnp.sum(jnp.sum(block, axis=0, keepdims=True), axis=1, keepdims=True)
    scale = 1.0 / (jnp.sqrt(trace) + 1e-07)
    for i in range(count):
        for part, value in enumerate(split_half(gram_ref[rows_of(i), :] * (scale * scale))):
            a_ref[part, rows_of(i), :] = value

    def step(k, carry):
        for i in range(count):
            width = side - i * SIDE
            now = a_ref[0, rows_of(i), i * SIDE :].astype(jnp.float32)
            now = now + a_ref[1, rows_of(i), i * SIDE :].astype(jnp.float32)
            strip = POLY_B * now + POLY_C * strip_of(a_ref, a_ref, i)
            put(p_ref, i, jnp.where(diagonal(i, width), strip + POLY_A, strip))

        @pl.when(k < NS_STEPS - 1)
        def _():
            for i in range(count):
                put(t_ref, i, strip_of(a_ref, p_ref, i))
            for i in range(count):
                put(a_ref, i, strip_of(t_ref, p_ref, i))

        there = lax.rem(k, 2)

        @pl.when(k == 0)
        def _():
            q_ref[0] = p_ref[...]

        @pl.when(k > 0)
        def _():
            for i in range(count):
                put(q_ref, i, strip_of(q_ref.at[1 - there], p_ref, i), (there,))

        return carry

    lax.fori_loop(0, NS_STEPS, step, 0)
    last = (NS_STEPS - 1) % 2
    for i in range(count):
        value = q_ref[last, 0, rows_of(i), :].astype(jnp.float32)
        value = (value + q_ref[last, 1, rows_of(i), :].astype(jnp.float32)) * scale
        high_ref[rows_of(i), :], low_ref[rows_of(i), :] = split_half(value)


def orthogonal_factor(gram):
    side = gram.shape[0]
    pair = (2, side, side)
    return pl.pallas_call(
        factor_kernel,
        out_shape=(jax.ShapeDtypeStruct(gram.shape, jnp.bfloat16),) * 2,
        scratch_shapes=[
            pltpu.VMEM(pair, jnp.bfloat16),
            pltpu.VMEM(pair, jnp.bfloat16),
            pltpu.VMEM(pair, jnp.bfloat16),
            pltpu.VMEM((2,) + pair, jnp.bfloat16),
        ],
        compiler_params=pltpu.CompilerParams(vmem_limit_bytes=56 * 1024 * 1024),
        cost_estimate=pl.CostEstimate(
            flops=17 * 4 * side**3, bytes_accessed=8 * side * side, transcendentals=0
        ),
    )(gram)


def body(tokens, cotangent, lengths, *rest):
    order = ("z", "v", "g", "phi", "h", "u", "up", "down")
    masters = dict(zip(order, rest[:8]))
    moments = dict(zip(order, rest[8:16]))
    channel_params, channel_moment, query_params, query_moment = rest[16:]
    seq_count = lax.axis_size("seq")
    seq_index = lax.axis_index("seq")
    dp_count = lax.axis_size("dp")
    dp_index = lax.axis_index("dp")
    rows = tokens.shape[0]

    half = {name: as_half(own_slice(masters[name])) for name in order}
    far_own = jnp.concatenate([half["up"], half["down"]], axis=0)
    far_held = jnp.stack([far_own] + others_blocks(far_own))
    cut = half["up"].shape[0]
    full = {"up": far_gather(far_held[:, :cut]), "down": far_gather(far_held[:, cut:])}
    small = jnp.concatenate(
        [
            channel_params,
            jnp.pad(query_params, ((0, channel_params.shape[0] - query_params.shape[0]), (0, 0))),
        ],
        axis=1,
    )
    small = as_half(small)
    small_all = in_order(small, others_blocks(small)).astype(jnp.float32)
    channel = small_all[:, : channel_params.shape[1]]
    query_set = small_all.reshape(seq_count, -1, small_all.shape[1])[
        :, : query_params.shape[0], channel_params.shape[1] :
    ].reshape(Z, 3)
    get_v = Flight(near_gather, [half["v"]], small)

    gain_one = channel[:, 0]
    gain_two = channel[:, 1]
    omega = channel[:, 2]
    alpha, delta, beta, eta = (
        channel[:, 3 + k * NE : 3 + (k + 1) * NE].T for k in range(4)
    )
    scale_q = query_set[:, 0]
    shift_q = query_set[:, 1]
    scale_k = query_set[:, 2]
    score_scale = Z ** (-0.5)

    place = seq_index * rows + jnp.arange(rows, dtype=jnp.int32)
    keep = (place < lengths[0]).astype(jnp.float32)[:, None]
    inputs = tokens.astype(jnp.float32)
    weighted = cotangent.astype(jnp.float32) * keep
    back_ffn = as_half(weighted)
    evens = [(i, i + 1) for i in range(0, seq_count - 1, 2)]
    odds = [(i + 1, i) for i in range(0, seq_count - 1, 2)]

    normed, norm_back_one = jax.vjp(norm_rows, inputs, gain_one)
    normed_low = as_half(normed)
    inject_rate = jax.nn.sigmoid(alpha)
    damp = jax.nn.sigmoid(delta)
    decay = 1.0 - inject_rate * damp
    mix = eta * inject_rate * beta
    decay_tiled, mix_tiled = tiled(decay), tiled(mix)
    decay_all = decay_tiled**rows
    normed_tiled = tiled(normed)
    ends = local_call(
        ema_end_kernel, f32_shape(NE, SUBS, LANES), 2 * rows * NE * D, 4 * rows * D, normed_tiled, decay_tiled
    )
    normed_there = lax.ppermute(normed_low, "seq", evens)
    clock = get_v.advance(ends)
    ends = clock
    zphi_slice = jnp.concatenate([half["z"], half["phi"]], axis=1)
    get_wide = Flight(whole_gather, [zphi_slice, half["h"]], clock)
    clock = get_v.advance(get_wide.beside)
    start = carried(ends, decay_all, True)
    clock = get_wide.advance(clock)
    clock = get_v.advance(clock)
    start, clock = tied(start, clock)
    ema_out = local_call(
        ema_run_kernel,
        f32_shape(rows, SUBS, LANES),
        4 * rows * NE * D,
        8 * rows * D,
        normed_tiled,
        decay_tiled,
        mix_tiled,
        start,
    )
    ema_out, clock = tied(ema_out, clock)
    clock = get_wide.advance(clock)
    clock = get_v.advance(clock)
    (full["v"],) = get_v.finish()
    normed_both = jnp.concatenate([normed_there, normed_low], axis=0)
    normed_both, clock = tied(normed_both, clock)
    v_pre = times_right(normed_both, full["v"])
    values_all = as_half(jax.nn.silu(v_pre))
    values_all, clock = tied(values_all, clock)
    clock = get_wide.advance(clock)
    get_near = Flight(near_gather, [half["g"], half["u"]], clock)
    clock = get_wide.advance(get_near.beside)
    zphi_full, full["h"] = get_wide.finish()
    full["z"], full["phi"] = zphi_full[:, :Z], zphi_full[:, Z:]
    ema_out, clock = tied(ema_out, clock)
    mix_pre = flat(ema_out) + omega * normed
    mixed_low = as_half(jax.nn.silu(mix_pre))
    z_pre = times_plain(mixed_low, full["z"])
    zed = jax.nn.silu(z_pre)
    queries_low = as_half(zed * scale_q + shift_q)
    keys_low = as_half(zed * scale_k)
    keys_there = lax.ppermute(keys_low, "seq", evens)
    phi = jax.nn.sigmoid(times_plain(mixed_low, full["phi"]))
    h_part = times_plain(mixed_low, full["h"])
    keys_there, h_part, clock = lax.optimization_barrier((keys_there, h_part, clock))
    clock = get_near.advance(clock)
    keys_all = jnp.concatenate([keys_there, keys_low], axis=0)
    odd_device = seq_index % 2 == 1
    query_place = jnp.arange(rows)[:, None]
    key_place = jnp.arange(2 * rows)[None, :]
    allowed = jnp.where(key_place < rows, odd_device, key_place - rows <= query_place)
    queries_low, clock = tied(queries_low, clock)
    scores = jnp.where(allowed, times_right(queries_low, keys_all) * score_scale, -1e30)
    top = jnp.max(scores, axis=-1, keepdims=True)
    expo = jnp.exp(scores - top)
    probs = expo / jnp.sum(expo, axis=-1, keepdims=True)
    probs_low = as_half(probs)
    attended = times_plain(probs_low, values_all)
    attended, clock = tied(attended, clock)
    clock = get_near.advance(clock)
    clock = get_near.advance(clock)
    clock = get_near.advance(clock)
    full["g"], full["u"] = get_near.finish()
    mixed_low, clock = tied(mixed_low, clock)
    gam_pre = times_right(mixed_low, full["g"])
    gamma = jax.nn.silu(gam_pre)
    gated_low = as_half(gamma * attended)
    h_pre = h_part + times_plain(gated_low, full["u"])
    cand = jax.nn.silu(h_pre)
    middle = phi * cand + (1.0 - phi) * inputs
    wide, norm_back_two = jax.vjp(norm_rows, middle, gain_two)
    wide_low = as_half(wide)
    a_pre = times_right(wide_low, full["up"])
    active_low = as_half(jax.nn.silu(a_pre))
    result = middle + times_plain(active_low, full["down"])
    block_output = as_half(result * keep)

    def share_of(name, total):
        return as_half(MOMENTUM * own_slice(moments[name]) + total)

    def kept_rows(shares):
        packed = jnp.concatenate([item.reshape(-1, D) for item in shares], axis=0)
        (packed,) = yield [packed], [lax.all_gather(packed, "dp", axis=0, tiled=False)]
        out, at = [], 0
        for item in shares:
            size = item.size // D
            out.append(packed[:, at : at + size].reshape(-1, item.shape[1]))
            at += size
        return out

    def column_rows(names, blocks):
        height = max(item.shape[0] for item in blocks)
        own = chosen(names, blocks, height)
        held = yield from in_columns(own, [SLOT[name] for name in names])
        return held

    def chosen(names, blocks, height):
        out = jnp.zeros((height, D), jnp.bfloat16)
        for name, item in zip(names, blocks):
            item = jnp.pad(item, ((0, height - item.shape[0]), (0, D - item.shape[1])))
            out = jnp.where(dp_index == SLOT[name], item, out)
        return out

    block = {}
    orders = chip_bits()

    clock = result
    grad = as_half(times_left(active_low, back_ffn))
    sum_down = Flight(far_sum, grad, clock)
    back_ffn, clock = tied(back_ffn, sum_down.beside)
    d_apre = as_half(times_right(back_ffn, full["down"]) * silu_grad(a_pre))
    d_apre, clock = tied(d_apre, clock)
    grad = as_half(times_left(d_apre, wide_low))
    sum_up = Flight(far_sum, grad, clock)
    clock = sum_up.beside
    d_apre, clock = tied(d_apre, clock)
    d_mid_norm, d_gain_two = norm_back_two(times_plain(d_apre, full["up"]))
    d_middle = weighted + d_mid_norm
    d_phipre = as_half(d_middle * (cand - inputs) * phi * (1.0 - phi))
    d_hpre = as_half(d_middle * phi * silu_grad(h_pre))
    tokens_grad = d_middle * (1.0 - phi)
    d_hpre, clock = tied(d_hpre, clock)
    grad = as_half(times_left(gated_low, d_hpre))
    sum_u = Flight(near_sum, grad, clock)
    d_hpre, clock = tied(d_hpre, sum_u.beside)
    d_gated = times_right(d_hpre, full["u"])
    d_attended = as_half(d_gated * gamma)
    d_gampre = as_half(d_gated * attended * silu_grad(gam_pre))
    d_gampre, clock = tied(d_gampre, clock)
    clock = sum_u.advance(clock)
    d_gampre, clock = tied(d_gampre, clock)
    grad = as_half(times_left(d_gampre, mixed_low))
    sum_g = Flight(near_sum, grad, clock)
    d_attended, clock = tied(d_attended, sum_g.beside)
    d_probs = times_right(d_attended, values_all)
    d_scores = as_half(probs * (d_probs - jnp.sum(probs * d_probs, axis=-1, keepdims=True)))
    d_scores, clock = tied(d_scores, clock)
    clock = sum_g.advance(clock)
    d_attended, clock = tied(d_attended, clock)
    d_vpre = as_half(times_left(probs_low, d_attended) * silu_grad(v_pre))
    d_vpre, clock = tied(d_vpre, clock)
    clock = sum_down.advance(clock)
    clock = sum_u.advance(clock)
    d_vpre, clock = tied(d_vpre, clock)
    grad = as_half(times_left(d_vpre, normed_both))
    sum_v = Flight(near_sum, grad, clock)
    d_vpre, clock = tied(d_vpre, sum_v.beside)
    d_queries = times_plain(d_scores, keys_all) * score_scale
    d_keys_all = times_left(d_scores, queries_low) * score_scale
    d_keys_there = lax.ppermute(d_keys_all[:rows], "seq", odds)
    d_normed_all = times_plain(d_vpre, full["v"])
    d_normed_there = lax.ppermute(as_half(d_normed_all[:rows]), "seq", odds)
    d_normed_all, clock = tied(d_normed_all, clock)
    clock = sum_v.advance(clock)
    clock = sum_g.advance(clock)
    clock = sum_down.advance(clock)
    keep_down = Flight(kept_rows, [share_of("down", sum_down.finish())], clock)
    clock = sum_up.advance(keep_down.beside)
    d_keys_there, clock = tied(d_keys_there, clock)
    d_keys = d_keys_all[rows:] + d_keys_there
    d_scale_q = jnp.sum(d_queries * zed, axis=0)
    d_shift_q = jnp.sum(d_queries, axis=0)
    d_scale_k = jnp.sum(d_keys * zed, axis=0)
    d_zpre = as_half((d_queries * scale_q + d_keys * scale_k) * silu_grad(z_pre))
    d_zphi = jnp.concatenate([d_zpre, d_phipre], axis=1)
    grads = [as_half(times_left(mixed_low, d_zphi)), as_half(times_left(mixed_low, d_hpre))]
    sum_wide = Flight(whole_sum, grads, clock)
    clock = sum_v.advance(sum_wide.beside)
    clock = sum_u.advance(clock)
    clock = sum_up.advance(clock)
    keep_up = Flight(kept_rows, [share_of("up", sum_up.finish())], clock)
    clock = sum_g.advance(keep_up.beside)
    clock = sum_wide.advance(clock)
    d_zphi, clock = tied(d_zphi, clock)
    d_mixed = (
        times_right(d_zphi, zphi_full)
        + times_right(d_hpre, full["h"])
        + times_plain(d_gampre, full["g"])
    )
    d_mixed, clock = tied(d_mixed, clock)
    clock = sum_v.advance(clock)
    clock = sum_g.advance(clock)
    clock = sum_wide.advance(clock)
    keep_near = Flight(
        kept_rows, [share_of("u", sum_u.finish()), share_of("g", sum_g.finish())], clock
    )
    clock = keep_down.advance(keep_near.beside)
    clock = keep_up.advance(clock)
    (block["down"],), (block["up"],) = keep_down.finish(), keep_up.finish()
    column_one = Flight(
        lambda x: column_rows(("down", "up"), x), [block["down"], block["up"]], clock
    )
    clock = sum_v.advance(column_one.beside)
    keep_v = Flight(kept_rows, [share_of("v", sum_v.finish())], clock)
    d_mixed, clock = tied(d_mixed, keep_v.beside)
    d_ema = d_mixed * silu_grad(mix_pre)
    d_ema_tiled = tiled(d_ema)
    state_shape = f32_shape(NE, SUBS, LANES)
    first, d_mix, d_state, state_tail = local_call(
        ema_sums_kernel,
        (state_shape,) * 4,
        10 * rows * NE * D,
        8 * rows * D,
        normed_tiled,
        d_ema_tiled,
        decay_tiled,
        start,
    )
    first, clock = tied(first, clock)
    clock = sum_wide.advance(clock)
    clock = column_one.advance(clock)
    behind = carried(first, decay_all, False)
    clock = keep_near.advance(clock)
    block["u"], block["g"] = keep_near.finish()
    clock = sum_wide.advance(clock)
    share_wide = sum_wide.finish()
    keep_wide = Flight(
        kept_rows,
        [
            share_of("phi", share_wide[:, Z : Z + D]),
            share_of("h", share_wide[:, Z + D :]),
            share_of("z", share_wide[:, :Z]),
        ],
        clock,
    )
    clock = keep_v.advance(keep_wide.beside)
    (block["v"],) = keep_v.finish()
    behind, clock = tied(behind, clock)
    d_normed_ema = flat(
        local_call(
            ema_back_kernel,
            f32_shape(rows, SUBS, LANES),
            4 * rows * NE * D,
            8 * rows * D,
            d_ema_tiled,
            decay_tiled,
            mix_tiled,
            behind,
        )
    )
    d_normed_ema, clock = tied(d_normed_ema, clock)
    clock = column_one.advance(clock)
    clock = keep_wide.advance(clock)
    block["phi"], block["h"], block["z"] = keep_wide.finish()
    column_two = Flight(lambda x: column_rows(("u", "g"), x), [block["u"], block["g"]], clock)
    column_three = Flight(
        lambda x: column_rows(("phi", "h", "z"), x),
        [block["phi"], block["h"], block["z"]],
        column_two.beside,
    )
    column_four = Flight(lambda x: column_rows(("v",), x), [block["v"]], column_three.beside)
    columns_held = [item.finish() for item in (column_one, column_two, column_three, column_four)]
    momentum = {name: block[name].astype(jnp.float32) for name in order}
    which = jnp.zeros((), jnp.int32)
    for index, names in enumerate(
        (("down", "up"), ("u", "g"), ("phi", "h", "z"), ("v",))
    ):
        for name in names:
            which = jnp.where(dp_index == SLOT[name], index, which)
    def gram_of(items):
        whole = jnp.concatenate(items, axis=0)
        return times_left(whole, whole)

    gram = lax.switch(
        which, [lambda *items, i=i: gram_of(items[i]) for i in range(4)], *columns_held
    )
    factor_high, factor_low = orthogonal_factor(gram)
    height = max(block[name].shape[0] for name in order)
    item = chosen(order, [block[name] for name in order], height)
    direction = as_half(times_plain(item, factor_high) + times_plain(item, factor_low))
    tall, middle_rows, low_rows = (size // seq_count for size in (FF, V, D))
    there = across(direction, 1)
    even = own_bit(1) == 0
    first_item, second_item = jnp.where(even, direction, there), jnp.where(even, there, direction)
    packed = jnp.where(
        dp_index < 4,
        jnp.concatenate([first_item[:tall], second_item[:low_rows]], axis=0),
        jnp.concatenate(
            [
                first_item[:middle_rows],
                second_item[:middle_rows],
                jnp.zeros((tall + low_rows - 2 * middle_rows, D), jnp.bfloat16),
            ],
            axis=0,
        ),
    )
    packed = pick(packed.reshape(2, -1, D), 0, own_bit(1))
    packed = lax.all_gather(packed, "dp", axis=0, tiled=True).reshape(-1, tall + low_rows, D)
    updated = {}
    for name in order:
        master = masters[name]
        chip, core = SLOT[name] // 2, SLOT[name] % 2
        at = 0 if core == 0 else (tall if chip < 2 else middle_rows)
        piece = packed[chip, at : at + master.shape[0], : master.shape[1]].astype(jnp.float32)
        rate = MATRIX_RATE * math.sqrt(master.shape[0] * seq_count / FAN[name])
        updated[name] = master - rate * piece

    d_normed_ema, direction = tied(d_normed_ema, direction)
    d_normed = d_normed_all[rows:] + d_normed_there.astype(jnp.float32)
    d_mix = flat(d_mix)
    d_decay = mix * flat(d_state + decay_tiled * behind * state_tail)
    d_eta = d_mix * inject_rate * beta
    d_beta = d_mix * eta * inject_rate
    d_inject = d_mix * eta * beta - d_decay * damp
    d_alpha = d_inject * inject_rate * (1.0 - inject_rate)
    d_delta = -d_decay * inject_rate * damp * (1.0 - damp)
    d_omega = jnp.sum(d_ema * normed, axis=0)
    d_input_norm, d_gain_one = norm_back_one(d_normed + d_normed_ema + omega * d_ema)
    tokens_grad = tokens_grad + d_input_norm

    query_rows = Z // seq_count
    grad_query = jnp.stack([d_scale_q, d_shift_q, d_scale_k]).reshape(3, seq_count, query_rows)
    grad_query = jnp.pad(grad_query, ((0, 0), (0, 0), (0, D // seq_count - query_rows)))
    small_sum = summed_small(
        jnp.concatenate(
            [
                d_gain_one[None],
                d_gain_two[None],
                d_omega[None],
                d_alpha,
                d_delta,
                d_beta,
                d_eta,
                grad_query.reshape(3, D),
            ],
            axis=0,
        )
    )
    columns = channel_params.shape[1]
    channel_renewed = MOMENTUM * channel_moment + small_sum[:columns].T
    query_renewed = MOMENTUM * query_moment + small_sum[columns:, :query_rows].T
    squares = jnp.concatenate(
        [
            jnp.sum(channel_renewed * channel_renewed, axis=0),
            jnp.sum(query_renewed * query_renewed, axis=0),
        ]
    )[None]
    squares = sum(others_blocks(squares), squares)[0]
    channel_rms = jnp.sqrt(squares[:columns] / D + 1e-06)
    channel_new = channel_params - VECTOR_RATE * channel_renewed / channel_rms
    query_rms = jnp.sqrt(squares[columns:] / Z + 1e-06)
    query_new = query_params - VECTOR_RATE * query_renewed / query_rms
    return (
        block_output,
        tokens_grad,
        *[updated[name] for name in order],
        *[momentum[name] for name in order],
        channel_new,
        channel_renewed,
        query_new,
        query_renewed,
    )


def solution(mesh):
    token_spec = P(("dp", "seq"), None)
    row_spec = P("seq", None)
    return jax.shard_map(
        body,
        mesh=mesh,
        in_specs=(token_spec, token_spec, P("dp")) + (row_spec,) * 20,
        out_specs=(token_spec, token_spec) + (row_spec,) * 20,
        check_vma=False,
    )
```
